256 devices in a mesh: wide: 128 (over x, z, y_lo, core), narrow: 2 (over y_hi).
Axes of the slice: x: 4, y: 4 (y_hi: 2, y_lo: 2; y = y_hi * 2 + y_lo), z: 8, core: 2. Of those that a mesh axis runs over, the one named last changes fastest.
Arguments:
- frames: bfloat16 [131072, 768], P(('wide', 'narrow')), may hold values from -6 to 6
- down_kernel: bfloat16 [15, 768], replicated, may hold values from -1.5 to 1.5
- proj_weight: bfloat16 [768, 1024], P('wide'), may hold values from -0.21875 to 0.21875
- glu_weight: bfloat16 [1024, 2, 1024], P('wide', None, 'narrow'), may hold values from -0.1875 to 0.1875
- conv_kernel: bfloat16 [15, 1024], P(None, 'narrow'), may hold values from -1.5 to 1.5
- conv_out_weight: bfloat16 [1024, 1024], P('narrow', 'wide'), may hold values from -0.5 to 0.5
- ffn_in: bfloat16 [1024, 4096], P('wide', 'narrow'), may hold values from -0.1875 to 0.1875
- ffn_out: bfloat16 [4096, 1024], P('narrow', 'wide'), may hold values from -0.25 to 0.25
Outputs:
- section_out: bfloat16 [65536, 1024], P(('wide', 'narrow'))
The draws below stay inside these ranges and needn't reach their ends.
All inputs are finite; a program needn't handle non-finite values.
Results may differ from the reference program's by a relative error of at most 0.017.
Values may be sent and summed in bfloat16 or wider, within the bound.
No kernel may reach another device: no remote copies, remote signals or barrier semaphores. Data moves between devices by JAX's collectives and lax.ppermute only.
A program may use at most 64 MiB of HBM per device.

```python
import math
import jax
import jax.numpy as jnp
from jax import lax

DIN = 768
D = 1024
FF = 4096
KERNEL = 15
FRAMES = 131072
RED = 65536


def block_levels(rng, dims, pieces, low, high):
    loudness, own = 1.0, jax.random.fold_in(rng, 6)
    for axis_at, shards_of in pieces:
        steps = jnp.exp(jax.random.uniform(jax.random.fold_in(own, axis_at), (shards_of,), jnp.float32, low / len(pieces), high / len(pieces)))
        loudness = loudness * jnp.repeat(steps, dims[axis_at] // shards_of).reshape([-1 if axis == axis_at else 1 for axis in range(len(dims))])
    return loudness


def gaussian(own_key, shape, deviation, bound, cuts=(), kind=jnp.bfloat16):
    level = block_levels(own_key, shape, cuts, -0.22, 0.18) if cuts else 1.0
    array = jax.random.normal(own_key, shape, jnp.float32) * deviation * level
    return jnp.minimum(jnp.maximum(array, -bound), bound).astype(kind)


def setup_inputs(seed: int = 0) -> dict:
    seeds = jax.random.split(jax.random.key(seed), 9)
    return {
        "frames": gaussian(seeds[0], (FRAMES, DIN), 1.0, 6.0, ((0, 256),)),
        "down_kernel": gaussian(seeds[1], (KERNEL, DIN), KERNEL ** -0.5, 1.5),
        "proj_weight": gaussian(seeds[2], (DIN, D), DIN ** -0.5, 0.21875, ((0, 128),)),
        "glu_weight": gaussian(seeds[3], (D, 2, D), D ** -0.5, 0.1875, ((0, 128), (2, 2))),
        "conv_kernel": gaussian(seeds[4], (KERNEL, D), KERNEL ** -0.5, 1.5, ((1, 2),)),
        "conv_out_weight": gaussian(seeds[5], (D, D), (D // 8) ** -0.5, 0.5, ((0, 2), (1, 128))),
        "ffn_in": gaussian(seeds[6], (D, FF), D ** -0.5, 0.1875, ((0, 128), (1, 2))),
        "ffn_out": gaussian(seeds[7], (FF, D), (FF // 8) ** -0.5, 0.25, ((0, 2), (1, 128))),
    }


def layer_norm(values):
    centre = lax.optimization_barrier(jnp.mean(values, axis=-1, keepdims=True))
    centred = values - centre
    spread = lax.optimization_barrier(jnp.mean(centred * centred, axis=-1, keepdims=True))
    return centred * lax.rsqrt(spread + 1e-05)

def reference(frames, down_kernel, proj_weight, glu_weight, conv_kernel, conv_out_weight, ffn_in, ffn_out):
    reach = KERNEL // 2
    padded = jnp.pad(frames.astype(jnp.float32), ((reach, reach), (0, 0)))
    reduced = jnp.zeros((RED, DIN), jnp.float32)
    for offset in range(KERNEL):
        window = lax.slice(padded, (offset, 0), (offset + FRAMES - 1, DIN), (2, 1))
        reduced = reduced + down_kernel[offset].astype(jnp.float32) * window
    reduced = reduced.astype(jnp.bfloat16)
    block = math.gcd(RED, 2048)
    count = RED // block
    glu_full = glu_weight.astype(jnp.float32)

    def front(rows):
        projected = jnp.dot(rows, proj_weight, preferred_element_type=jnp.float32).astype(jnp.bfloat16)
        normed = layer_norm(projected.astype(jnp.float32)).astype(jnp.bfloat16)
        glu_pre = jnp.einsum('rc,cgh->rgh', normed.astype(jnp.float32), glu_full)
        gated = (glu_pre[:, 0, :] * jax.nn.sigmoid(glu_pre[:, 1, :])).astype(jnp.bfloat16)
        return (projected, gated)
    projected, gated = lax.map(front, reduced.reshape(count, block, DIN))
    projected = projected.reshape(RED, D)
    gated = gated.reshape(RED, D)
    gated_pad = jnp.pad(gated.astype(jnp.float32), ((reach, reach), (0, 0)))
    depth = jnp.zeros((RED, D), jnp.float32)
    for offset in range(KERNEL):
        depth = depth + conv_kernel[offset].astype(jnp.float32) * gated_pad[offset:offset + RED]
    activated = jax.nn.silu(depth).astype(jnp.bfloat16)

    def back(pair):
        proj_rows, act_rows = pair
        mixed = proj_rows.astype(jnp.float32) + jnp.dot(act_rows, conv_out_weight, preferred_element_type=jnp.float32)
        second_norm = layer_norm(mixed).astype(jnp.bfloat16)
        hidden = jax.nn.silu(jnp.dot(second_norm, ffn_in, preferred_element_type=jnp.float32)).astype(jnp.bfloat16)
        result = mixed + 0.5 * jnp.dot(hidden, ffn_out, preferred_element_type=jnp.float32)
        return result.astype(jnp.bfloat16)
    section_out = lax.map(back, (projected.reshape(count, block, D), activated.reshape(count, block, D)))
    return section_out.reshape(RED, D)
```

```python
import functools

import jax
import jax.numpy as jnp
from jax import lax
from jax.experimental import pallas as pl
from jax.experimental.pallas import tpu as pltpu
from jax.sharding import Mesh
from jax.sharding import PartitionSpec as P

X, Z, YL, CORE, YH = 4, 8, 2, 2, 2
ALL = ("x", "z", "yl", "c", "yh")
WIDE = ("x", "z", "yl", "c")
Y = ("yl", "yh")
TAPS, REACH, PAD = 15, 7, 8
ROWS, DIN, D = 256, 768, 1024
WITH_HALO = ROWS + 2 * PAD
EDGE = 32
BF16, F32 = jnp.bfloat16, jnp.float32
ANY = pl.BlockSpec(memory_space=pl.ANY)
VMEM = pl.BlockSpec(memory_space=pltpu.VMEM)
SMEM = pl.BlockSpec(memory_space=pltpu.SMEM)


def params(mib=40):
    return pltpu.CompilerParams(vmem_limit_bytes=mib * 2**20)


def cost(flops, moved):
    return pl.CostEstimate(flops=flops, bytes_accessed=moved, transcendentals=0)


def from_offset(block, axis, offset):
    peers = lax.axis_size(axis)
    index = [0, 2, 1, 3] if axis == Y else range(peers)
    pairs = [(index[j], index[(j - offset) % peers]) for j in range(peers)]
    return lax.ppermute(block, axis, pairs)


def ring4(block, axis):
    half = block.shape[0] // 2
    after = from_offset(block, axis, 1)
    before = from_offset(block, axis, -1)
    low = from_offset(after[:half], axis, 1)
    high = from_offset(before[half:], axis, -1)
    full = block.shape[0]
    return [(0, 0, full, block), (1, 0, full, after), (3, 0, full, before),
            (2, 0, half, low), (2, half, half, high)]


def ring8(block, axis):
    half, full = block.shape[0] // 2, block.shape[0]
    pieces = [(0, 0, full, block)]
    after = before = block
    for step in range(1, 4):
        after = from_offset(after, axis, 1)
        before = from_offset(before, axis, -1)
        pieces += [(step, 0, full, after), (8 - step, 0, full, before)]
    low = from_offset(after[:half], axis, 1)
    high = from_offset(before[half:], axis, -1)
    return pieces + [(4, 0, half, low), (4, half, half, high)]


def direct(block, axis):
    peers, full = lax.axis_size(axis), block.shape[0]
    order = sorted(range(1, peers), key=lambda k: -min(k, peers - k))
    return [(0, 0, full, block)] + [
        (k, 0, full, from_offset(block, axis, k)) for k in order
    ]


def place(pieces, me, peers, out_shape, view):
    offsets = [(k, start, rows) for k, start, rows, _ in pieces]

    def kernel(me_ref, *refs):
        ins, out, sems = refs[: len(offsets)], refs[len(offsets)], refs[-1]
        copies = []
        for i, (k, start, rows) in enumerate(offsets):
            at = lax.rem(me_ref[0] + k, peers)
            copies.append(pltpu.make_async_copy(ins[i], view(out, at, start, rows), sems.at[i]))
        for copy in copies:
            copy.start()
        for copy in copies:
            copy.wait()

    blocks = [p for *_, p in pieces]
    moved = 2 * sum(2 * b.size for b in blocks)
    return pl.pallas_call(
        kernel,
        out_shape=jax.ShapeDtypeStruct(out_shape, BF16),
        in_specs=[SMEM] + [ANY] * len(blocks),
        out_specs=ANY,
        scratch_shapes=[pltpu.SemaphoreType.DMA((len(blocks),))],
        compiler_params=params(4),
        cost_estimate=cost(0, moved),
    )(me, *blocks)


def layer_norm(values):
    centre = jnp.mean(values, axis=-1, keepdims=True)
    centred = values - centre
    spread = jnp.mean(centred * centred, axis=-1, keepdims=True)
    return centred * lax.rsqrt(spread + 1e-05)


def reduce_kernel(before_ref, frames_ref, after_ref, taps_ref, out_ref, wide):
    rows = frames_ref.shape[0]
    columns = []
    for j in range(DIN // 128):
        lanes = slice(j * 128, (j + 1) * 128)
        wide[j, 0:EDGE] = before_ref[:, lanes].astype(F32)
        wide[j, EDGE : EDGE + rows] = frames_ref[:, lanes].astype(F32)
        wide[j, EDGE + rows :] = after_ref[:, lanes].astype(F32)
        total = jnp.zeros((WITH_HALO, 128), F32)
        for k in range(TAPS):
            start = EDGE - 2 * PAD - REACH + k
            window = wide[j, pl.ds(start, WITH_HALO, stride=2), :]
            total = total + taps_ref[k : k + 1, lanes].astype(F32) * window
        columns.append(total.astype(BF16))
    reduced = jnp.concatenate(columns, axis=1)
    lane = lax.broadcasted_iota(jnp.int32, (DIN, D), 1)
    row = lax.broadcasted_iota(jnp.int32, (DIN, D), 0)
    source = (lane >> 3) * 6 + (lane & 7)
    spread = jnp.where((source == row) & ((lane & 7) < 6), 1.0, 0.0).astype(BF16)
    out_ref[...] = jnp.dot(reduced, spread, preferred_element_type=F32).astype(BF16)


def dot_t(a, b):
    return lax.dot_general(a, b, (((1,), (1,)), ((), ())), preferred_element_type=F32)


def load_kernel_copies(refs, views, sems):
    copies = [
        pltpu.make_async_copy(ref, view, sems.at[i])
        for i, (ref, view) in enumerate(zip(refs, views, strict=True))
    ]
    for copy in copies:
        copy.start()
    return copies


def front_kernel(offsets, info_ref, reduced_ref, taps_ref, *refs):
    n = len(offsets)
    own, other = refs[:n], refs[n : 2 * n]
    mixed_ref, norm_ref, weights, gated_ref, sems = refs[2 * n :]
    x, core = info_ref[0], info_ref[1]

    def views(side):
        out = []
        for k, start, rows in offsets:
            out.append(weights.at[side, pl.ds(start, rows), lax.rem(x + k, X)])
        return out

    copies = load_kernel_copies(own + other, views(core) + views(1 - core), sems)
    for copy in copies:
        copy.wait()

    def mat(side, yh):
        return weights[side, yh].reshape(D, D)

    reduced = reduced_ref[...]
    projected = jnp.concatenate(
        [jnp.dot(reduced, mat(1, yh)[:, 512:], preferred_element_type=F32).astype(BF16) for yh in range(YH)], axis=1)
    projected = projected.astype(F32)
    normed = layer_norm(projected).astype(BF16)
    row = lax.broadcasted_iota(jnp.int32, (WITH_HALO, 1), 0)
    inside = (row >= info_ref[2]) & (row < info_ref[3])
    mixed = projected[PAD : PAD + ROWS]
    for yh in range(YH):
        pre = jnp.dot(normed, mat(0, yh), preferred_element_type=F32)
        gated = (pre[:, :512] * jax.nn.sigmoid(pre[:, 512:])).astype(BF16).astype(F32)
        gated_ref[...] = jnp.where(inside, gated, 0.0)
        depth = jnp.zeros((ROWS, 512), F32)
        for k in range(TAPS):
            tap = taps_ref[k : k + 1, yh * 512 : (yh + 1) * 512].astype(F32)
            depth = depth + tap * gated_ref[pl.ds(PAD - REACH + k, ROWS), :]
        activated = jax.nn.silu(depth).astype(BF16)
        mixed = mixed + dot_t(activated, mat(1, yh)[:, :512])
    mixed_ref[...] = mixed
    norm_ref[...] = layer_norm(mixed).astype(BF16)


def hidden_kernel(offsets, info_ref, own_ref, other_ref, *refs):
    n = len(offsets)
    pieces, (own_out, other_out, weights, sems) = refs[:n], refs[n:]
    y = info_ref[0]
    views = []
    for k, start, rows in offsets:
        at = lax.rem(y + k, YH * YL)
        views.append(weights.at[at // YL, pl.ds(start, rows), :, at % YL])
    for copy in load_kernel_copies(pieces, views, sems):
        copy.wait()
    for yh in range(YH):
        matrix = weights[yh].reshape(D, D)
        for src, out in ((other_ref, other_out), (own_ref, own_out)):
            pre = jnp.dot(src[...], matrix, preferred_element_type=F32)
            out[yh] = jax.nn.silu(pre).astype(BF16)


def out_kernel(offsets, info_ref, hidden_ref, *refs):
    n = len(offsets)
    pieces, (out_ref, weights, sems) = refs[:n], refs[n:]
    z = info_ref[0]
    views = [
        weights.at[pl.ds(start, rows), :, lax.rem(z + k, Z)] for k, start, rows in offsets
    ]
    for copy in load_kernel_copies(pieces, views, sems):
        copy.wait()
    total = dot_t(hidden_ref[0], weights[0].reshape(D, D))
    total = total + dot_t(hidden_ref[1], weights[1].reshape(D, D))
    out_ref[...] = total.astype(out_ref.dtype)


def body(frames, down, proj, glu, conv_taps, conv_out, ffn_in, ffn_out):
    core, x, z = lax.axis_index("c"), lax.axis_index("x"), lax.axis_index("z")
    y = lax.axis_index("yh") * YL + lax.axis_index("yl")
    where = lax.axis_index(ALL)
    yh = lax.axis_index("yh")

    def scalars(*values):
        return jnp.stack([jnp.asarray(v, jnp.int32) for v in values])

    proj_half = lax.dynamic_slice_in_dim(proj, yh * 512, 512, 1)
    proj_half = jnp.pad(proj_half, ((0, 2), (0, 0)))
    half_a = [glu.reshape(8, 1024), ffn_in[:, :1024], ffn_out.T[:, :1024]]
    half_b = [jnp.concatenate([conv_out.T, proj_half], axis=1), ffn_in[:, 1024:], ffn_out.T[:, 1024:]]
    half_a, half_b = jnp.stack(half_a), jnp.stack(half_b)
    mine = jnp.where(core == 0, half_a, half_b)
    theirs = from_offset(jnp.where(core == 0, half_b, half_a), "c", 1)
    block = jnp.concatenate(
        [jnp.where(core == 0, mine, theirs), jnp.where(core == 0, theirs, mine)], axis=1
    )
    peers = lax.axis_size(ALL)
    before = lax.ppermute(frames[-EDGE:], ALL, [(i, i + 1) for i in range(peers - 1)])
    after = lax.ppermute(frames[:EDGE], ALL, [(i + 1, i) for i in range(peers - 1)])
    taps_other = from_offset(conv_taps, "yh", 1)
    taps = jnp.where(
        yh == 0,
        jnp.concatenate([conv_taps, taps_other], axis=1),
        jnp.concatenate([taps_other, conv_taps], axis=1),
    )

    first = place(
        direct(block[0:2], "z"), scalars(z), Z, (2, Z, 16, D),
        lambda out, at, start, rows: out.at[:, at],
    )
    out_first = place(
        direct(block[2:3], "x"), scalars(x), X, (1, X, 16, D),
        lambda out, at, start, rows: out.at[:, at],
    )
    front_second = place(
        ring4(first[0], Y), scalars(y), 4, (YH, Z, YL, 16, D),
        lambda out, at, start, rows: out.at[at // YL, pl.ds(start, rows), at % YL],
    )
    in_second = place(
        ring4(first[1], "x"), scalars(x), X, (X, Z, 16, D),
        lambda out, at, start, rows: out.at[at, pl.ds(start, rows)],
    )
    out_second = place(
        ring4(out_first[0], Y), scalars(y), 4, (YH, X, YL, 16, D),
        lambda out, at, start, rows: out.at[at // YL, pl.ds(start, rows), at % YL],
    )
    front_pieces = ring4(front_second, "x")
    in_pieces = ring4(in_second, Y)
    out_pieces = ring8(out_second, "z")
    front_other = [from_offset(p, "c", 1) for *_, p in front_pieces]

    reduced = pl.pallas_call(
        reduce_kernel,
        out_shape=jax.ShapeDtypeStruct((WITH_HALO, D), BF16),
        in_specs=[VMEM] * 4,
        out_specs=VMEM,
        scratch_shapes=[pltpu.VMEM((DIN // 128, 2 * EDGE + frames.shape[0], 128), F32)],
        compiler_params=params(24),
        cost_estimate=cost(2 * WITH_HALO * DIN * D, 10**7),
    )(before, frames, after, down)

    low = jnp.where(where == 0, PAD, 0)
    high = jnp.where(where == peers - 1, PAD + ROWS, WITH_HALO)
    offsets = [p[:3] for p in front_pieces]
    mixed, norm = pl.pallas_call(
        functools.partial(front_kernel, offsets),
        out_shape=(jax.ShapeDtypeStruct((ROWS, D), F32), jax.ShapeDtypeStruct((ROWS, D), BF16)),
        in_specs=[SMEM, VMEM, VMEM] + [ANY] * (2 * len(offsets)),
        out_specs=(VMEM, VMEM),
        scratch_shapes=[
            pltpu.VMEM((2, YH, X, Z, YL, 16, D), BF16),
            pltpu.VMEM((WITH_HALO, 512), F32),
            pltpu.SemaphoreType.DMA((2 * len(offsets),)),
        ],
        compiler_params=params(),
        cost_estimate=cost(2 * WITH_HALO * D * D * 4, 10**7),
    )(scalars(x, core, low, high), reduced, taps, *[p[3] for p in front_pieces], *front_other)

    norm_other = from_offset(norm, "c", 1)
    offsets = [p[:3] for p in in_pieces]
    hidden_shape = jax.ShapeDtypeStruct((YH, ROWS, D), BF16)
    hidden_own, hidden_other = pl.pallas_call(
        functools.partial(hidden_kernel, offsets),
        out_shape=(hidden_shape, hidden_shape),
        in_specs=[SMEM, VMEM, VMEM] + [ANY] * len(offsets),
        out_specs=(VMEM, VMEM),
        scratch_shapes=[
            pltpu.VMEM((YH, X, Z, YL, 16, D), BF16),
            pltpu.SemaphoreType.DMA((len(offsets),)),
        ],
        compiler_params=params(),
        cost_estimate=cost(4 * 2 * ROWS * D * D, 10**7),
    )(scalars(y), norm, norm_other, *[p[3] for p in in_pieces])

    offsets = [p[:3] for p in out_pieces]

    def product(hidden, dtype):
        return pl.pallas_call(
            functools.partial(out_kernel, offsets),
            out_shape=jax.ShapeDtypeStruct((ROWS, D), dtype),
            in_specs=[SMEM, VMEM] + [ANY] * len(offsets),
            out_specs=VMEM,
            scratch_shapes=[
                pltpu.VMEM((YH, X, Z, YL, 16, D), BF16),
                pltpu.SemaphoreType.DMA((len(offsets),)),
            ],
            compiler_params=params(),
            cost_estimate=cost(2 * 2 * ROWS * D * D, 10**7),
        )(scalars(z), hidden, *[p[3] for p in out_pieces])

    share = from_offset(product(hidden_other, BF16), "c", 1)
    return (mixed + 0.5 * (product(hidden_own, F32) + share.astype(F32))).astype(BF16)


def solution(mesh):
    parts = Mesh(mesh.devices.reshape(X, Z, YL, CORE, YH), ALL)
    return jax.shard_map(
        body,
        mesh=parts,
        in_specs=(
            P(ALL, None),
            P(),
            P(WIDE, None),
            P(WIDE, None, "yh"),
            P(None, "yh"),
            P("yh", WIDE),
            P(WIDE, "yh"),
            P("yh", WIDE),
        ),
        out_specs=P(ALL, None),
        check_vma=False,
    )
```

```python
import functools
import itertools

import jax
import jax.numpy as jnp
from jax import lax
from jax.experimental import pallas as pl
from jax.experimental.pallas import tpu as pltpu
from jax.sharding import Mesh
from jax.sharding import PartitionSpec as P

X, Z, YL, CORE, YH = 4, 8, 2, 2, 2
ALL = ("x", "z", "yl", "c", "yh")
WIDE = ("x", "z", "yl", "c")
Y = ("yl", "yh")
TAPS, REACH, PAD = 15, 7, 8
ROWS, DIN, D = 256, 768, 1024
WITH_HALO = ROWS + 2 * PAD
EDGE = 32
BF16, F32 = jnp.bfloat16, jnp.float32
ANY = pl.BlockSpec(memory_space=pl.ANY)
VMEM = pl.BlockSpec(memory_space=pltpu.VMEM)
SMEM = pl.BlockSpec(memory_space=pltpu.SMEM)


def params(mib=40):
    return pltpu.CompilerParams(vmem_limit_bytes=mib * 2**20)


def cost(flops, moved):
    return pl.CostEstimate(flops=flops, bytes_accessed=moved, transcendentals=0)


def from_offset(block, axis, offset):
    peers = lax.axis_size(axis)
    index = [0, 2, 1, 3] if axis == Y else range(peers)
    pairs = [(index[j], index[(j - offset) % peers]) for j in range(peers)]
    return lax.ppermute(block, axis, pairs)


def ring8(block, axis):
    half, full = block.shape[0] // 2, block.shape[0]
    pieces = [(0, 0, full, block)]
    after = before = block
    for step in range(1, 4):
        after = from_offset(after, axis, 1)
        before = from_offset(before, axis, -1)
        pieces += [(step, 0, full, after), (8 - step, 0, full, before)]
    low = from_offset(after[:half], axis, 1)
    high = from_offset(before[half:], axis, -1)
    return pieces + [(4, 0, half, low), (4, half, half, high)]


def direct4(block, axis):
    full = block.shape[0]
    return [(0, 0, full, block)] + [
        (k, 0, full, from_offset(block, axis, k)) for k in (2, 1, 3)
    ]


def crossed(block, offset, x_core):
    pairs = []
    for x, y, core in itertools.product(range(X), range(YL * YH), range(CORE)):
        to = ((x - offset) % X, y) if core == x_core else (x, (y - offset) % (YL * YH))
        index = [((i * YL + j % YL) * CORE + core) * YH + j // YL for i, j in ((x, y), to)]
        pairs.append(tuple(index))
    return lax.ppermute(block, ("x", "yl", "c", "yh"), pairs)


def middle_ring(block):
    after, before = crossed(block, 1, 1), crossed(block, -1, 1)
    full = block.shape[0]
    return [(0, 0, full, block), (1, 0, full, after), (3, 0, full, before),
            (2, 0, full, crossed(after, 1, 1))]


def last_ring(block, between=None):
    half, full = block.shape[0] // 2, block.shape[0]
    after, before = crossed(block, 1, 0), crossed(block, -1, 0)
    low, high = after[:half], before[half:]
    if between is not None:
        low, high, between = lax.optimization_barrier((low, high, between))
    low, high = crossed(low, 1, 0), crossed(high, -1, 0)
    return [(0, 0, full, block), (1, 0, full, after), (3, 0, full, before),
            (2, 0, half, low), (2, half, half, high)], between


def spread_z(block, core):
    after, before = from_offset(block, "z", 1), from_offset(block, "z", -1)
    two_after = from_offset(jnp.stack([block, after]), "z", 2)
    two_before = from_offset(jnp.stack([block, before]), "z", -2)
    pairs = []
    for z, c in itertools.product(range(Z), range(CORE)):
        to = (z - 3) % Z if c == 0 else (z + 3) % Z
        pairs.append((z * CORE + c, to * CORE + c))
    far = lax.ppermute(jnp.where(core == 0, after, before), ("z", "c"), pairs)
    return [(0, 0, 1, block[None]), (1, 0, 1, after[None]), (7, 0, 1, before[None]),
            (2, 0, 2, two_after), (6, 0, -2, two_before), (4, 0, 1, far[None])]


def place(pieces, info, plan, out_shapes):
    count = len(plan([0] * info.shape[0]))

    def kernel(info_ref, *refs):
        ins, outs, sems = refs[: len(pieces)], refs[len(pieces) : -1], refs[-1]
        copies = []
        for i, (piece, part, out, at) in enumerate(plan(info_ref)):
            source = ins[piece] if part is None else ins[piece].at[part]
            copies.append(pltpu.make_async_copy(source, outs[out].at[at], sems.at[i]))
        for copy in copies:
            copy.start()
        for copy in copies:
            copy.wait()

    moved = 2 * sum(2 * b.size for b in pieces)
    return pl.pallas_call(
        kernel,
        out_shape=[jax.ShapeDtypeStruct(s, BF16) for s in out_shapes],
        in_specs=[SMEM] + [ANY] * len(pieces),
        out_specs=[ANY] * len(out_shapes),
        scratch_shapes=[pltpu.SemaphoreType.DMA((count,))],
        compiler_params=params(4),
        cost_estimate=cost(0, moved),
    )(info, *pieces)


def layer_norm(values):
    centre = jnp.mean(values, axis=-1, keepdims=True)
    centred = values - centre
    spread = jnp.mean(centred * centred, axis=-1, keepdims=True)
    return centred * lax.rsqrt(spread + 1e-05)


def reduce_kernel(before_ref, frames_ref, after_ref, taps_ref, out_ref, wide):
    rows = frames_ref.shape[0]
    columns = []
    for j in range(DIN // 128):
        lanes = slice(j * 128, (j + 1) * 128)
        wide[j, 0:EDGE] = before_ref[:, lanes].astype(F32)
        wide[j, EDGE : EDGE + rows] = frames_ref[:, lanes].astype(F32)
        wide[j, EDGE + rows :] = after_ref[:, lanes].astype(F32)
        total = jnp.zeros((WITH_HALO, 128), F32)
        for k in range(TAPS):
            start = EDGE - 2 * PAD - REACH + k
            window = wide[j, pl.ds(start, WITH_HALO, stride=2), :]
            total = total + taps_ref[k : k + 1, lanes].astype(F32) * window
        columns.append(total.astype(BF16))
    reduced = jnp.concatenate(columns, axis=1)
    lane = lax.broadcasted_iota(jnp.int32, (DIN, D), 1)
    row = lax.broadcasted_iota(jnp.int32, (DIN, D), 0)
    source = (lane >> 3) * 6 + (lane & 7)
    spread = jnp.where((source == row) & ((lane & 7) < 6), 1.0, 0.0).astype(BF16)
    out_ref[...] = jnp.dot(reduced, spread, preferred_element_type=F32).astype(BF16)


def dot_t(a, b):
    return lax.dot_general(a, b, (((1,), (1,)), ((), ())), preferred_element_type=F32)


def start_copies(pairs, sems):
    copies = [
        pltpu.make_async_copy(source, target, sems.at[i])
        for i, (source, target) in enumerate(pairs)
    ]
    for copy in copies:
        copy.start()
    return copies


def crossed_copies(refs, offsets, weights, x, y, core):
    pairs = []
    last = jnp.where(core == 0, x, y)
    for ref, (k, start, rows) in zip(refs, offsets, strict=True):
        at = lax.rem(last + k, 4)
        for m in range(rows):
            to_x = jnp.where(core == 0, at, start + m)
            to_y = jnp.where(core == 0, start + m, at)
            pairs.append((ref.at[m], weights.at[to_y // YL, to_x, :, lax.rem(to_y, YL)]))
    return pairs


def front_kernel(offsets, info_ref, reduced_ref, *refs):
    n = len(offsets)
    own, other = refs[:n], refs[n : 2 * n]
    mixed_ref, norm_ref, weights, gated_ref, sems = refs[2 * n :]
    x, y, core = info_ref[0], info_ref[1], info_ref[2]
    pairs = crossed_copies(own, offsets, weights.at[core], x, y, core)
    pairs += crossed_copies(other, offsets, weights.at[1 - core], x, y, 1 - core)
    for copy in start_copies(pairs, sems):
        copy.wait()

    def mat(side, yh):
        return weights[side, yh].reshape(D, D)

    reduced = reduced_ref[...]
    projected = jnp.concatenate(
        [jnp.dot(reduced, mat(1, yh)[:, 512:], preferred_element_type=F32).astype(BF16) for yh in range(YH)], axis=1)
    projected = projected.astype(F32)
    normed = layer_norm(projected).astype(BF16)
    row = lax.broadcasted_iota(jnp.int32, (WITH_HALO, 1), 0)
    inside = (row >= info_ref[3]) & (row < info_ref[4])
    mixed = projected[PAD : PAD + ROWS]
    for yh in range(YH):
        pre = jnp.dot(normed, mat(0, yh), preferred_element_type=F32)
        gated = (pre[:, :512] * jax.nn.sigmoid(pre[:, 512:])).astype(BF16).astype(F32)
        gated_ref[...] = jnp.where(inside, gated, 0.0)
        depth = jnp.zeros((ROWS, 512), F32)
        for k in range(TAPS):
            tap_rows = weights[1, yh, 0, k // 8, (k // 4) % 2][:, 512:].astype(F32)
            at = 8 * ((k // 2) % 2) + 6 + k % 2
            tap = tap_rows[at : at + 1]
            depth = depth + tap * gated_ref[pl.ds(PAD - REACH + k, ROWS), :]
        activated = jax.nn.silu(depth).astype(BF16)
        mixed = mixed + dot_t(activated, mat(1, yh)[:, :512])
    mixed_ref[...] = mixed
    norm_ref[...] = layer_norm(mixed).astype(BF16)


def hidden_kernel(offsets, info_ref, own_ref, other_ref, *refs):
    n = len(offsets)
    pieces, (own_out, other_out, weights, sems) = refs[:n], refs[n:]
    pairs = crossed_copies(pieces, offsets, weights, info_ref[0], info_ref[1], info_ref[2])
    for copy in start_copies(pairs, sems):
        copy.wait()
    for yh in range(YH):
        matrix = weights[yh].reshape(D, D)
        for src, out in ((other_ref, other_out), (own_ref, own_out)):
            pre = jnp.dot(src[...], matrix, preferred_element_type=F32)
            out[yh] = jax.nn.silu(pre).astype(BF16)


def out_kernel(offsets, info_ref, hidden_ref, *refs):
    n = len(offsets)
    pieces, (out_ref, weights, sems) = refs[:n], refs[n:]
    z = info_ref[5]
    pairs = [
        (ref, weights.at[pl.ds(start, rows), :, lax.rem(z + k, Z)])
        for ref, (k, start, rows) in zip(pieces, offsets, strict=True)
    ]
    for copy in start_copies(pairs, sems):
        copy.wait()
    total = dot_t(hidden_ref[0], weights[0].reshape(D, D))
    total = total + dot_t(hidden_ref[1], weights[1].reshape(D, D))
    out_ref[...] = total.astype(out_ref.dtype)


def body(frames, down, proj, glu, conv_taps, conv_out, ffn_in, ffn_out):
    core, x, z = lax.axis_index("c"), lax.axis_index("x"), lax.axis_index("z")
    yh, yl = lax.axis_index("yh"), lax.axis_index("yl")
    y = yh * YL + yl
    where = lax.axis_index(ALL)
    peers = lax.axis_size(ALL)

    proj_half = lax.dynamic_slice_in_dim(proj, yh * 512, 512, 1)
    taps_at = 2 * (lax.rem(z, 2) * 4 + yl * 2 + core)
    taps = lax.dynamic_slice_in_dim(jnp.pad(conv_taps, ((0, 1), (0, 0))), taps_at, 2, 0)
    proj_half = jnp.concatenate([proj_half, taps], axis=0)
    half_a = [glu.reshape(8, 1024), ffn_in[:, :1024], ffn_out.T[:, :1024]]
    half_b = [jnp.concatenate([conv_out.T, proj_half], axis=1), ffn_in[:, 1024:], ffn_out.T[:, 1024:]]
    half_a, half_b = jnp.stack(half_a), jnp.stack(half_b)
    mine = jnp.where(core == 0, half_a, half_b)
    theirs = from_offset(jnp.where(core == 0, half_b, half_a), "c", 1)
    before = lax.ppermute(frames[-EDGE:], ALL, [(i, i + 1) for i in range(peers - 1)])
    after = lax.ppermute(frames[:EDGE], ALL, [(i + 1, i) for i in range(peers - 1)])
    theirs, before, after = lax.optimization_barrier((theirs, before, after))
    block = jnp.concatenate(
        [jnp.where(core == 0, mine, theirs), jnp.where(core == 0, theirs, mine)], axis=1
    )
    info = jnp.stack(
        [x, y, core, jnp.where(where == 0, PAD, 0),
         jnp.where(where == peers - 1, PAD + ROWS, WITH_HALO), z, jnp.where(core == 0, y, x)]
    ).astype(jnp.int32)

    reduced = pl.pallas_call(
        reduce_kernel,
        out_shape=jax.ShapeDtypeStruct((WITH_HALO, D), BF16),
        in_specs=[VMEM] * 4,
        out_specs=VMEM,
        scratch_shapes=[pltpu.VMEM((DIN // 128, 2 * EDGE + frames.shape[0], 128), F32)],
        compiler_params=params(24),
        cost_estimate=cost(2 * WITH_HALO * DIN * D, 10**7),
    )(before, frames, after, down)

    pieces = spread_z(block[:2], core)
    out_pieces = direct4(block[2], "x")

    def plan_z(info_ref):
        steps = []
        for i, (k, _, rows, _) in enumerate(pieces):
            for j in range(abs(rows)):
                at = lax.rem(info_ref[5] + k + (j if rows > 0 else -j), Z)
                steps.append((i, j, 0, (slice(None), at)))
        return steps

    def plan_x(info_ref):
        return [(i, None, 0, lax.rem(info_ref[0] + k, X)) for i, (k, *_) in enumerate(out_pieces)]

    (first,) = place([p[3] for p in pieces], info, plan_z, [(2, Z, 16, D)])
    (out_first,) = place([p[3] for p in out_pieces], info, plan_x, [(X, 16, D)])
    middle = middle_ring(first)
    out_pieces = direct4(out_first, Y)

    def plan_middle(info_ref):
        return [
            (i, half, half, lax.rem(info_ref[6] + k, 4))
            for half in range(2)
            for i, (k, *_) in enumerate(middle)
        ]

    def plan_y(info_ref):
        steps = []
        for i, (k, *_) in enumerate(out_pieces):
            at = lax.rem(info_ref[1] + k, 4)
            steps.append((i, None, 0, (at // YL, slice(None), lax.rem(at, YL))))
        return steps

    front_block, in_block = place([p[3] for p in middle], info, plan_middle, [(4, Z, 16, D)] * 2)
    (out_second,) = place([p[3] for p in out_pieces], info, plan_y, [(YH, X, YL, 16, D)])
    front_pieces, reduced = last_ring(front_block, reduced)
    out_pieces = ring8(out_second, "z")
    in_pieces, _ = last_ring(in_block)
    front_other = [from_offset(p, "c", 1) for *_, p in front_pieces]

    offsets = [p[:3] for p in front_pieces]
    mixed, norm = pl.pallas_call(
        functools.partial(front_kernel, offsets),
        out_shape=(jax.ShapeDtypeStruct((ROWS, D), F32), jax.ShapeDtypeStruct((ROWS, D), BF16)),
        in_specs=[SMEM, VMEM] + [ANY] * (2 * len(offsets)),
        out_specs=(VMEM, VMEM),
        scratch_shapes=[
            pltpu.VMEM((2, YH, X, Z, YL, 16, D), BF16),
            pltpu.VMEM((WITH_HALO, 512), F32),
            pltpu.SemaphoreType.DMA((32,)),
        ],
        compiler_params=params(),
        cost_estimate=cost(2 * WITH_HALO * D * D * 4, 10**7),
    )(info, reduced, *[p[3] for p in front_pieces], *front_other)

    norm_other = from_offset(norm, "c", 1)
    offsets = [p[:3] for p in in_pieces]
    hidden_shape = jax.ShapeDtypeStruct((YH, ROWS, D), BF16)
    hidden_own, hidden_other = pl.pallas_call(
        functools.partial(hidden_kernel, offsets),
        out_shape=(hidden_shape, hidden_shape),
        in_specs=[SMEM, VMEM, VMEM] + [ANY] * len(offsets),
        out_specs=(VMEM, VMEM),
        scratch_shapes=[
            pltpu.VMEM((YH, X, Z, YL, 16, D), BF16),
            pltpu.SemaphoreType.DMA((16,)),
        ],
        compiler_params=params(),
        cost_estimate=cost(4 * 2 * ROWS * D * D, 10**7),
    )(info, norm, norm_other, *[p[3] for p in in_pieces])

    offsets = [p[:3] for p in out_pieces]

    def product(hidden, dtype):
        return pl.pallas_call(
            functools.partial(out_kernel, offsets),
            out_shape=jax.ShapeDtypeStruct((ROWS, D), dtype),
            in_specs=[SMEM, VMEM] + [ANY] * len(offsets),
            out_specs=VMEM,
            scratch_shapes=[
                pltpu.VMEM((YH, X, Z, YL, 16, D), BF16),
                pltpu.SemaphoreType.DMA((len(offsets),)),
            ],
            compiler_params=params(),
            cost_estimate=cost(2 * 2 * ROWS * D * D, 10**7),
        )(info, hidden, *[p[3] for p in out_pieces])

    share = from_offset(product(hidden_other, BF16), "c", 1)
    return (mixed + 0.5 * (product(hidden_own, F32) + share.astype(F32))).astype(BF16)


def solution(mesh):
    parts = Mesh(mesh.devices.reshape(X, Z, YL, CORE, YH), ALL)
    return jax.shard_map(
        body,
        mesh=parts,
        in_specs=(
            P(ALL, None),
            P(),
            P(WIDE, None),
            P(WIDE, None, "yh"),
            P(None, "yh"),
            P("yh", WIDE),
            P(WIDE, "yh"),
            P("yh", WIDE),
        ),
        out_specs=P(ALL, None),
        check_vma=False,
    )
```

```python
import functools
import itertools

import jax
import jax.numpy as jnp
from jax import lax
from jax.experimental import pallas as pl
from jax.experimental.pallas import tpu as pltpu
from jax.sharding import Mesh
from jax.sharding import PartitionSpec as P

X, Z, YL, CORE, YH = 4, 8, 2, 2, 2
ALL = ("x", "z", "yl", "c", "yh")
WIDE = ("x", "z", "yl", "c")
Y = ("yl", "yh")
TAPS, REACH, PAD = 15, 7, 8
ROWS, DIN, D = 256, 768, 1024
WITH_HALO = ROWS + 2 * PAD
EDGE = 32
BF16, F32 = jnp.bfloat16, jnp.float32
ANY = pl.BlockSpec(memory_space=pl.ANY)
VMEM = pl.BlockSpec(memory_space=pltpu.VMEM)
SMEM = pl.BlockSpec(memory_space=pltpu.SMEM)


def params(mib=20):
    return pltpu.CompilerParams(vmem_limit_bytes=mib * 2**20)


def cost(flops, moved):
    return pl.CostEstimate(flops=flops, bytes_accessed=moved, transcendentals=0)


def from_offset(block, axis, offset):
    peers = lax.axis_size(axis)
    index = [0, 2, 1, 3] if axis == Y else range(peers)
    pairs = [(index[j], index[(j - offset) % peers]) for j in range(peers)]
    return lax.ppermute(block, axis, pairs)


def crossed(block, offset, x_core):
    pairs = []
    for x, y, core in itertools.product(range(X), range(YL * YH), range(CORE)):
        to = ((x - offset) % X, y) if core == x_core else (x, (y - offset) % (YL * YH))
        index = [((i * YL + j % YL) * CORE + core) * YH + j // YL for i, j in ((x, y), to)]
        pairs.append(tuple(index))
    return lax.ppermute(block, ("x", "yl", "c", "yh"), pairs)


def middle_ring(block):
    after, before = crossed(block, 1, 1), crossed(block, -1, 1)
    full = block.shape[0]
    return [(0, 0, full, block), (1, 0, full, after), (3, 0, full, before),
            (2, 0, full, crossed(after, 1, 1))]


def last_ring(block):
    half, full = block.shape[0] // 2, block.shape[0]
    after, before = crossed(block, 1, 0), crossed(block, -1, 0)

    def rest(low, high):
        low, high = crossed(low, 1, 0), crossed(high, -1, 0)
        return [(0, 0, full, block), (1, 0, full, after), (3, 0, full, before),
                (2, 0, half, low), (2, half, half, high)]

    return after[:half], before[half:], rest


def one_way_z(block):
    pairs = []
    for z, core in itertools.product(range(Z), range(CORE)):
        to = (z - 1) % Z if core == 0 else (z + 1) % Z
        pairs.append((z * CORE + core, to * CORE + core))
    return lax.ppermute(block, ("z", "c"), pairs)


def spread_z(block, core):
    after, before = from_offset(block, "z", 1), from_offset(block, "z", -1)
    two_after = from_offset(jnp.stack([block, after]), "z", 2)
    two_before = from_offset(jnp.stack([block, before]), "z", -2)
    pairs = []
    for z, c in itertools.product(range(Z), range(CORE)):
        to = (z - 3) % Z if c == 0 else (z + 3) % Z
        pairs.append((z * CORE + c, to * CORE + c))
    far = lax.ppermute(jnp.where(core == 0, after, before), ("z", "c"), pairs)
    return [(0, 0, 1, block[None]), (1, 0, 1, after[None]), (7, 0, 1, before[None]),
            (2, 0, 2, two_after), (6, 0, -2, two_before), (4, 0, 1, far[None])]


def place(pieces, info, plan, out_shapes):
    count = len(plan([0] * info.shape[0]))

    def kernel(info_ref, *refs):
        ins, outs, sems = refs[: len(pieces)], refs[len(pieces) : -1], refs[-1]
        copies = []
        for i, (piece, part, out, at) in enumerate(plan(info_ref)):
            source = ins[piece] if part is None else ins[piece].at[part]
            copies.append(pltpu.make_async_copy(source, outs[out].at[at], sems.at[i]))
        for copy in copies:
            copy.start()
        for copy in copies:
            copy.wait()

    moved = 2 * sum(2 * b.size for b in pieces)
    return pl.pallas_call(
        kernel,
        out_shape=[jax.ShapeDtypeStruct(s, BF16) for s in out_shapes],
        in_specs=[SMEM] + [ANY] * len(pieces),
        out_specs=[ANY] * len(out_shapes),
        scratch_shapes=[pltpu.SemaphoreType.DMA((count,))],
        compiler_params=params(4),
        cost_estimate=cost(0, moved),
    )(info, *pieces)


def layer_norm(values):
    centre = jnp.mean(values, axis=-1, keepdims=True)
    centred = values - centre
    spread = jnp.mean(centred * centred, axis=-1, keepdims=True)
    return centred * lax.rsqrt(spread + 1e-05)


def reduce_kernel(before_ref, frames_ref, after_ref, taps_ref, out_ref, wide):
    rows = frames_ref.shape[0]
    columns = []
    for j in range(DIN // 128):
        lanes = slice(j * 128, (j + 1) * 128)
        wide[j, 0:EDGE] = before_ref[:, lanes].astype(F32)
        wide[j, EDGE : EDGE + rows] = frames_ref[:, lanes].astype(F32)
        wide[j, EDGE + rows :] = after_ref[:, lanes].astype(F32)
        total = jnp.zeros((WITH_HALO, 128), F32)
        for k in range(TAPS):
            start = EDGE - 2 * PAD - REACH + k
            window = wide[j, pl.ds(start, WITH_HALO, stride=2), :]
            total = total + taps_ref[k : k + 1, lanes].astype(F32) * window
        columns.append(total.astype(BF16))
    reduced = jnp.concatenate(columns, axis=1)
    lane = lax.broadcasted_iota(jnp.int32, (DIN, D), 1)
    row = lax.broadcasted_iota(jnp.int32, (DIN, D), 0)
    source = (lane >> 3) * 6 + (lane & 7)
    spread = jnp.where((source == row) & ((lane & 7) < 6), 1.0, 0.0).astype(BF16)
    out_ref[...] = jnp.dot(reduced, spread, preferred_element_type=F32).astype(BF16)


def dot_t(a, b):
    return lax.dot_general(a, b, (((1,), (1,)), ((), ())), preferred_element_type=F32)


def start_copies(pairs, sems):
    copies = [
        pltpu.make_async_copy(source, target, sems.at[i])
        for i, (source, target) in enumerate(pairs)
    ]
    for copy in copies:
        copy.start()
    return copies


def crossed_copies(refs, offsets, weights, x, y, core):
    pairs = []
    last = jnp.where(core == 0, x, y)
    for ref, (k, start, rows) in zip(refs, offsets, strict=True):
        at = lax.rem(last + k, 4)
        for m in range(rows):
            to_x = jnp.where(core == 0, at, start + m)
            to_y = jnp.where(core == 0, start + m, at)
            pairs.append((ref.at[m], weights.at[to_y // YL, to_x, :, lax.rem(to_y, YL)]))
    return pairs


def front_kernel(offsets, info_ref, reduced_ref, *refs):
    n = len(offsets)
    own, other = refs[:n], refs[n : 2 * n]
    mixed_ref, norm_ref, weights, gated_ref, sems = refs[2 * n :]
    x, y, core = info_ref[0], info_ref[1], info_ref[2]
    pairs = crossed_copies(own, offsets, weights.at[core], x, y, core)
    pairs += crossed_copies(other, offsets, weights.at[1 - core], x, y, 1 - core)
    for copy in start_copies(pairs, sems):
        copy.wait()

    def mat(side, yh):
        return weights[side, yh].reshape(D, D)

    reduced = reduced_ref[...]
    projected = jnp.concatenate(
        [jnp.dot(reduced, mat(1, yh)[:, 512:], preferred_element_type=F32).astype(BF16) for yh in range(YH)], axis=1)
    projected = projected.astype(F32)
    normed = layer_norm(projected).astype(BF16)
    row = lax.broadcasted_iota(jnp.int32, (WITH_HALO, 1), 0)
    inside = (row >= info_ref[3]) & (row < info_ref[4])
    mixed = projected[PAD : PAD + ROWS]
    for yh in range(YH):
        pre = jnp.dot(normed, mat(0, yh), preferred_element_type=F32)
        gated = (pre[:, :512] * jax.nn.sigmoid(pre[:, 512:])).astype(BF16).astype(F32)
        gated_ref[...] = jnp.where(inside, gated, 0.0)
        depth = jnp.zeros((ROWS, 512), F32)
        for k in range(TAPS):
            tap_rows = weights[1, yh, 0, k // 8, (k // 4) % 2][:, 512:].astype(F32)
            at = 8 * ((k // 2) % 2) + 6 + k % 2
            tap = tap_rows[at : at + 1]
            depth = depth + tap * gated_ref[pl.ds(PAD - REACH + k, ROWS), :]
        activated = jax.nn.silu(depth).astype(BF16)
        mixed = mixed + dot_t(activated, mat(1, yh)[:, :512])
    mixed_ref[...] = mixed
    norm_ref[...] = layer_norm(mixed).astype(BF16)


def hidden_of(rows, weights, yh):
    pre = jnp.dot(rows, weights[yh].reshape(D, D), preferred_element_type=F32)
    return jax.nn.silu(pre).astype(BF16)


def out_copies(refs, weights, z, core, sems):
    pairs = []
    for k, ref in enumerate(refs):
        at = lax.rem(z + jnp.where(core == 0, k, Z - k), Z)
        pairs.append((ref, weights.at[:, :, at]))
    return start_copies(pairs, sems)


def other_kernel(offsets, info_ref, own_ref, other_ref, *refs):
    n = len(offsets)
    pieces, out_pieces = refs[:n], refs[n : n + Z]
    hidden_ref, share_ref, first, second, sems, out_sems = refs[n + Z :]
    pairs = crossed_copies(pieces, offsets, first, info_ref[0], info_ref[1], info_ref[2])
    copies = start_copies(pairs, sems)
    later = out_copies(out_pieces, second, info_ref[5], info_ref[2], out_sems)
    for copy in copies:
        copy.wait()
    hidden = [hidden_of(other_ref[...], first, yh) for yh in range(YH)]
    for yh in range(YH):
        hidden_ref[yh] = hidden_of(own_ref[...], first, yh)
    for copy in later:
        copy.wait()
    total = dot_t(hidden[0], second[0].reshape(D, D))
    share_ref[...] = (total + dot_t(hidden[1], second[1].reshape(D, D))).astype(BF16)


def own_kernel(info_ref, hidden_ref, mixed_ref, *refs):
    out_pieces, (out_ref, second, out_sems) = refs[:Z], refs[Z:]
    for copy in out_copies(out_pieces, second, info_ref[5], info_ref[2], out_sems):
        copy.wait()
    total = dot_t(hidden_ref[0], second[0].reshape(D, D))
    total = total + dot_t(hidden_ref[1], second[1].reshape(D, D))
    out_ref[...] = mixed_ref[...] + 0.5 * total


def body(frames, down, proj, glu, conv_taps, conv_out, ffn_in, ffn_out):
    core, x, z = lax.axis_index("c"), lax.axis_index("x"), lax.axis_index("z")
    yh, yl = lax.axis_index("yh"), lax.axis_index("yl")
    y = yh * YL + yl
    where = lax.axis_index(ALL)
    peers = lax.axis_size(ALL)

    proj_half = lax.dynamic_slice_in_dim(proj, yh * 512, 512, 1)
    taps_at = 2 * (lax.rem(z, 2) * 4 + yl * 2 + core)
    taps = lax.dynamic_slice_in_dim(jnp.pad(conv_taps, ((0, 1), (0, 0))), taps_at, 2, 0)
    proj_half = jnp.concatenate([proj_half, taps], axis=0)
    half_a = jnp.stack([glu.reshape(8, 1024), ffn_in[:, :1024]])
    half_b = jnp.stack([jnp.concatenate([conv_out.T, proj_half], axis=1), ffn_in[:, 1024:]])
    mine = jnp.where(core == 0, half_a, half_b)
    theirs = from_offset(jnp.where(core == 0, half_b, half_a), "c", 1)
    out_halves = jnp.stack([ffn_out.T[:, :1024], ffn_out.T[:, 1024:]])
    out_halves = jnp.broadcast_to(out_halves[:, None], (X, YL, CORE, YH, 8, D))
    out_plane = lax.all_to_all(
        out_halves.reshape(-1, 8, D), ("x", "yl", "c", "yh"), 0, 0, tiled=True
    )
    block = jnp.concatenate(
        [jnp.where(core == 0, mine, theirs), jnp.where(core == 0, theirs, mine)], axis=1
    )
    info = jnp.stack(
        [x, y, core, jnp.where(where == 0, PAD, 0),
         jnp.where(where == peers - 1, PAD + ROWS, WITH_HALO), z, jnp.where(core == 0, y, x)]
    ).astype(jnp.int32)

    pieces = spread_z(block, core)

    def plan_z(info_ref):
        steps = []
        for i, (k, _, rows, _) in enumerate(pieces):
            for j in range(abs(rows)):
                at = lax.rem(info_ref[5] + k + (j if rows > 0 else -j), Z)
                steps.append((i, j, 0, (slice(None), at)))
        return steps

    z_blocks, out_plane = lax.optimization_barrier(([p[3] for p in pieces], out_plane))
    out_plane = out_plane.reshape(X, YL, CORE, YH, 8, D).transpose(3, 0, 1, 2, 4, 5)
    out_pieces = [out_plane.reshape(YH, X, YL, 16, D)]

    def more_out(steps):
        for _ in range(steps):
            out_pieces.append(one_way_z(out_pieces[-1]))

    more_out(2)
    (first,) = place(z_blocks, info, plan_z, [(2, Z, 16, D)])
    middle = middle_ring(first)

    def plan_middle(info_ref):
        return [
            (i, half, half, lax.rem(info_ref[6] + k, 4))
            for half in range(2)
            for i, (k, *_) in enumerate(middle)
        ]

    frames, first = lax.optimization_barrier((frames, first))
    pairs = [(i, i ^ 1) for i in range(peers)]
    start, end = frames[:EDGE], frames[-EDGE:]
    near = lax.ppermute(jnp.where(yh == 0, end, start), ALL, pairs)
    pairs = [(i, j) for i in range(peers) if 0 <= (j := i + 2 * (i % 2) - 1) < peers]
    far = lax.ppermute(jnp.where(yh == 0, start, end), ALL, pairs)
    before, after = jnp.where(yh == 0, far, near), jnp.where(yh == 0, near, far)
    blocks, out_pieces[-1], before, after = lax.optimization_barrier(
        ([p[3] for p in middle], out_pieces[-1], before, after)
    )
    front_block, in_block = place(blocks, info, plan_middle, [(4, Z, 16, D)] * 2)
    front_low, front_high, front_rest = last_ring(front_block)
    in_low, in_high, in_rest = last_ring(in_block)
    more_out(3)
    front_low, front_high, in_low, in_high, out_pieces[-1] = lax.optimization_barrier(
        (front_low, front_high, in_low, in_high, out_pieces[-1])
    )
    more_out(2)
    reduced = pl.pallas_call(
        reduce_kernel,
        out_shape=jax.ShapeDtypeStruct((WITH_HALO, D), BF16),
        in_specs=[VMEM] * 4,
        out_specs=VMEM,
        scratch_shapes=[pltpu.VMEM((DIN // 128, 2 * EDGE + frames.shape[0], 128), F32)],
        compiler_params=params(12),
        cost_estimate=cost(2 * WITH_HALO * DIN * D, 10**7),
    )(before, frames, after, down)
    front_pieces = front_rest(front_low, front_high)
    in_pieces = in_rest(in_low, in_high)
    front_other = [from_offset(p, "c", 1) for *_, p in front_pieces]

    offsets = [p[:3] for p in front_pieces]
    mixed, norm = pl.pallas_call(
        functools.partial(front_kernel, offsets),
        out_shape=(jax.ShapeDtypeStruct((ROWS, D), F32), jax.ShapeDtypeStruct((ROWS, D), BF16)),
        in_specs=[SMEM, VMEM] + [ANY] * (2 * len(offsets)),
        out_specs=(VMEM, VMEM),
        scratch_shapes=[
            pltpu.VMEM((2, YH, X, Z, YL, 16, D), BF16),
            pltpu.VMEM((WITH_HALO, 512), F32),
            pltpu.SemaphoreType.DMA((32,)),
        ],
        compiler_params=params(),
        cost_estimate=cost(2 * WITH_HALO * D * D * 4, 10**7),
    )(info, reduced, *[p[3] for p in front_pieces], *front_other)

    norm_other = from_offset(norm, "c", 1)
    offsets = [p[:3] for p in in_pieces]
    whole = pltpu.VMEM((YH, X, Z, YL, 16, D), BF16)
    hidden, share = pl.pallas_call(
        functools.partial(other_kernel, offsets),
        out_shape=(
            jax.ShapeDtypeStruct((YH, ROWS, D), BF16),
            jax.ShapeDtypeStruct((ROWS, D), BF16),
        ),
        in_specs=[SMEM, VMEM, VMEM] + [ANY] * (len(offsets) + Z),
        out_specs=(VMEM, VMEM),
        scratch_shapes=[
            whole, whole, pltpu.SemaphoreType.DMA((16,)), pltpu.SemaphoreType.DMA((Z,))
        ],
        compiler_params=params(),
        cost_estimate=cost(6 * 2 * ROWS * D * D, 10**7),
    )(info, norm, norm_other, *[p[3] for p in in_pieces], *out_pieces)
    share = from_offset(share, "c", 1)
    own = pl.pallas_call(
        own_kernel,
        out_shape=jax.ShapeDtypeStruct((ROWS, D), F32),
        in_specs=[SMEM, VMEM, VMEM] + [ANY] * Z,
        out_specs=VMEM,
        scratch_shapes=[whole, pltpu.SemaphoreType.DMA((Z,))],
        compiler_params=params(),
        cost_estimate=cost(2 * 2 * ROWS * D * D, 10**7),
    )(info, hidden, mixed, *out_pieces)
    return (own + 0.5 * share.astype(F32)).astype(BF16)


def solution(mesh):
    parts = Mesh(mesh.devices.reshape(X, Z, YL, CORE, YH), ALL)
    return jax.shard_map(
        body,
        mesh=parts,
        in_specs=(
            P(ALL, None),
            P(),
            P(WIDE, None),
            P(WIDE, None, "yh"),
            P(None, "yh"),
            P("yh", WIDE),
            P(WIDE, "yh"),
            P("yh", WIDE),
        ),
        out_specs=P(ALL, None),
        check_vma=False,
    )
```

```python
import functools
import itertools

import jax
import jax.numpy as jnp
from jax import lax
from jax.experimental import pallas as pl
from jax.experimental.pallas import tpu as pltpu
from jax.sharding import Mesh
from jax.sharding import PartitionSpec as P

X, Z, YL, CORE, YH = 4, 8, 2, 2, 2
ALL = ("x", "z", "yl", "c", "yh")
WIDE = ("x", "z", "yl", "c")
Y = ("yl", "yh")
TAPS, REACH, PAD = 15, 7, 8
ROWS, DIN, D = 256, 768, 1024
WITH_HALO = ROWS + 2 * PAD
EDGE = 32
BF16, F32 = jnp.bfloat16, jnp.float32
ANY = pl.BlockSpec(memory_space=pl.ANY)
VMEM = pl.BlockSpec(memory_space=pltpu.VMEM)
SMEM = pl.BlockSpec(memory_space=pltpu.SMEM)


def params(mib=20):
    return pltpu.CompilerParams(vmem_limit_bytes=mib * 2**20)


def cost(flops, moved):
    return pl.CostEstimate(flops=flops, bytes_accessed=moved, transcendentals=0)


def from_offset(block, axis, offset):
    peers = lax.axis_size(axis)
    index = [0, 2, 1, 3] if axis == Y else range(peers)
    pairs = [(index[j], index[(j - offset) % peers]) for j in range(peers)]
    return lax.ppermute(block, axis, pairs)


def crossed(block, offset, x_core):
    pairs = []
    for x, y, core in itertools.product(range(X), range(YL * YH), range(CORE)):
        to = ((x - offset) % X, y) if core == x_core else (x, (y - offset) % (YL * YH))
        index = [((i * YL + j % YL) * CORE + core) * YH + j // YL for i, j in ((x, y), to)]
        pairs.append(tuple(index))
    return lax.ppermute(block, ("x", "yl", "c", "yh"), pairs)


def middle_ring(block):
    after, before = crossed(block, 1, 1), crossed(block, -1, 1)
    full = block.shape[0]
    return [(0, 0, full, block), (1, 0, full, after), (3, 0, full, before),
            (2, 0, full, crossed(after, 1, 1))]


def last_ring(block):
    half, full = block.shape[0] // 2, block.shape[0]
    after, before = crossed(block, 1, 0), crossed(block, -1, 0)

    def rest(low, high):
        low, high = crossed(low, 1, 0), crossed(high, -1, 0)
        return [(0, 0, full, block), (1, 0, full, after), (3, 0, full, before),
                (2, 0, half, low), (2, half, half, high)]

    return after[:half], before[half:], rest


def one_way_z(block):
    pairs = []
    for z, core in itertools.product(range(Z), range(CORE)):
        to = (z - 1) % Z if core == 0 else (z + 1) % Z
        pairs.append((z * CORE + core, to * CORE + core))
    return lax.ppermute(block, ("z", "c"), pairs)


def spread_z(block, core):
    after, before = from_offset(block, "z", 1), from_offset(block, "z", -1)
    two_after = from_offset(jnp.stack([block, after]), "z", 2)
    two_before = from_offset(jnp.stack([block, before]), "z", -2)
    pairs = []
    for z, c in itertools.product(range(Z), range(CORE)):
        to = (z - 3) % Z if c == 0 else (z + 3) % Z
        pairs.append((z * CORE + c, to * CORE + c))
    far = lax.ppermute(jnp.where(core == 0, after, before), ("z", "c"), pairs)
    return [(0, 0, 1, block[None]), (1, 0, 1, after[None]), (7, 0, 1, before[None]),
            (2, 0, 2, two_after), (6, 0, -2, two_before), (4, 0, 1, far[None])]


def place(pieces, info, plan, out_shapes):
    count = len(plan([0] * info.shape[0]))

    def kernel(info_ref, *refs):
        ins, outs, sems = refs[: len(pieces)], refs[len(pieces) : -1], refs[-1]
        copies = []
        for i, (piece, part, out, at) in enumerate(plan(info_ref)):
            source = ins[piece] if part is None else ins[piece].at[part]
            copies.append(pltpu.make_async_copy(source, outs[out].at[at], sems.at[i]))
        for copy in copies:
            copy.start()
        for copy in copies:
            copy.wait()

    moved = 2 * sum(2 * b.size for b in pieces)
    return pl.pallas_call(
        kernel,
        out_shape=[jax.ShapeDtypeStruct(s, BF16) for s in out_shapes],
        in_specs=[SMEM] + [ANY] * len(pieces),
        out_specs=[ANY] * len(out_shapes),
        scratch_shapes=[pltpu.SemaphoreType.DMA((count,))],
        compiler_params=params(4),
        cost_estimate=cost(0, moved),
    )(info, *pieces)


def layer_norm(values):
    centre = jnp.mean(values, axis=-1, keepdims=True)
    centred = values - centre
    spread = jnp.mean(centred * centred, axis=-1, keepdims=True)
    return centred * lax.rsqrt(spread + 1e-05)


def reduce_kernel(before_ref, frames_ref, after_ref, taps_ref, out_ref, wide):
    rows = frames_ref.shape[0]
    columns = []
    for j in range(DIN // 128):
        lanes = slice(j * 128, (j + 1) * 128)
        wide[j, 0:EDGE] = before_ref[:, lanes].astype(F32)
        wide[j, EDGE : EDGE + rows] = frames_ref[:, lanes].astype(F32)
        wide[j, EDGE + rows :] = after_ref[:, lanes].astype(F32)
        total = jnp.zeros((WITH_HALO, 128), F32)
        for k in range(TAPS):
            start = EDGE - 2 * PAD - REACH + k
            window = wide[j, pl.ds(start, WITH_HALO, stride=2), :]
            total = total + taps_ref[k : k + 1, lanes].astype(F32) * window
        columns.append(total.astype(BF16))
    reduced = jnp.concatenate(columns, axis=1)
    lane = lax.broadcasted_iota(jnp.int32, (DIN, D), 1)
    row = lax.broadcasted_iota(jnp.int32, (DIN, D), 0)
    source = (lane >> 3) * 6 + (lane & 7)
    spread = jnp.where((source == row) & ((lane & 7) < 6), 1.0, 0.0).astype(BF16)
    out_ref[...] = jnp.dot(reduced, spread, preferred_element_type=F32).astype(BF16)


def dot_t(a, b):
    return lax.dot_general(a, b, (((1,), (1,)), ((), ())), preferred_element_type=F32)


def start_copies(pairs, sems):
    copies = [
        pltpu.make_async_copy(source, target, sems.at[i])
        for i, (source, target) in enumerate(pairs)
    ]
    for copy in copies:
        copy.start()
    return copies


def crossed_copies(refs, offsets, weights, x, y, core):
    pairs = []
    last = jnp.where(core == 0, x, y)
    for ref, (k, start, rows) in zip(refs, offsets, strict=True):
        at = lax.rem(last + k, 4)
        for m in range(rows):
            to_x = jnp.where(core == 0, at, start + m)
            to_y = jnp.where(core == 0, start + m, at)
            pairs.append((ref.at[m], weights.at[to_y // YL, to_x, :, lax.rem(to_y, YL)]))
    return pairs


def front_kernel(offsets, info_ref, reduced_ref, *refs):
    n = len(offsets)
    own, other = refs[:n], refs[n : 2 * n]
    mixed_ref, norm_ref, weights, gated_ref, sems = refs[2 * n :]
    x, y, core = info_ref[0], info_ref[1], info_ref[2]
    pairs = crossed_copies(own, offsets, weights.at[core], x, y, core)
    pairs += crossed_copies(other, offsets, weights.at[1 - core], x, y, 1 - core)
    for copy in start_copies(pairs, sems):
        copy.wait()

    def mat(side, yh):
        return weights[side, yh].reshape(D, D)

    reduced = reduced_ref[...]
    projected = jnp.concatenate(
        [jnp.dot(reduced, mat(1, yh)[:, 512:], preferred_element_type=F32).astype(BF16) for yh in range(YH)], axis=1)
    projected = projected.astype(F32)
    normed = layer_norm(projected).astype(BF16)
    row = lax.broadcasted_iota(jnp.int32, (WITH_HALO, 1), 0)
    inside = (row >= info_ref[3]) & (row < info_ref[4])
    mixed = projected[PAD : PAD + ROWS]
    for yh in range(YH):
        pre = jnp.dot(normed, mat(0, yh), preferred_element_type=F32)
        gated = (pre[:, :512] * jax.nn.sigmoid(pre[:, 512:])).astype(BF16).astype(F32)
        gated_ref[...] = jnp.where(inside, gated, 0.0)
        depth = jnp.zeros((ROWS, 512), F32)
        for k in range(TAPS):
            tap_rows = weights[1, yh, 0, k // 8, (k // 4) % 2][:, 512:].astype(F32)
            at = 8 * ((k // 2) % 2) + 6 + k % 2
            tap = tap_rows[at : at + 1]
            depth = depth + tap * gated_ref[pl.ds(PAD - REACH + k, ROWS), :]
        activated = jax.nn.silu(depth).astype(BF16)
        mixed = mixed + dot_t(activated, mat(1, yh)[:, :512])
    mixed_ref[...] = mixed
    norm_ref[...] = layer_norm(mixed).astype(BF16)


def hidden_of(rows, weights, yh):
    pre = jnp.dot(rows, weights[yh].reshape(D, D), preferred_element_type=F32)
    return jax.nn.silu(pre).astype(BF16)


def out_copies(refs, weights, z, core, sems):
    pairs = []
    for k, ref in enumerate(refs):
        at = lax.rem(z + jnp.where(core == 0, k, Z - k), Z)
        pairs.append((ref, weights.at[:, :, at]))
    return start_copies(pairs, sems)


def other_kernel(offsets, info_ref, own_ref, other_ref, *refs):
    n = len(offsets)
    pieces, out_pieces = refs[:n], refs[n : n + Z]
    hidden_ref, share_ref, first, second, sems, out_sems = refs[n + Z :]
    pairs = crossed_copies(pieces, offsets, first, info_ref[0], info_ref[1], info_ref[2])
    copies = start_copies(pairs, sems)
    later = out_copies(out_pieces, second, info_ref[5], info_ref[2], out_sems)
    for copy in copies:
        copy.wait()
    hidden = [hidden_of(other_ref[...], first, yh) for yh in range(YH)]
    for yh in range(YH):
        hidden_ref[yh] = hidden_of(own_ref[...], first, yh)
    for copy in later:
        copy.wait()
    total = dot_t(hidden[0], second[0].reshape(D, D))
    share_ref[...] = (total + dot_t(hidden[1], second[1].reshape(D, D))).astype(BF16)


def own_kernel(info_ref, hidden_ref, mixed_ref, *refs):
    out_pieces, (out_ref, second, out_sems) = refs[:Z], refs[Z:]
    for copy in out_copies(out_pieces, second, info_ref[5], info_ref[2], out_sems):
        copy.wait()
    total = dot_t(hidden_ref[0], second[0].reshape(D, D))
    total = total + dot_t(hidden_ref[1], second[1].reshape(D, D))
    out_ref[...] = mixed_ref[...] + 0.5 * total


def body(frames, down, proj, glu, conv_taps, conv_out, ffn_in, ffn_out):
    core, x, z = lax.axis_index("c"), lax.axis_index("x"), lax.axis_index("z")
    yh, yl = lax.axis_index("yh"), lax.axis_index("yl")
    y = yh * YL + yl
    where = lax.axis_index(ALL)
    peers = lax.axis_size(ALL)

    proj_half = lax.dynamic_slice_in_dim(proj, yh * 512, 512, 1)
    taps_at = 2 * (lax.rem(z, 2) * 4 + yl * 2 + core)
    taps = lax.dynamic_slice_in_dim(jnp.pad(conv_taps, ((0, 1), (0, 0))), taps_at, 2, 0)
    proj_half = jnp.concatenate([proj_half, taps], axis=0)
    half_a = jnp.stack([glu.reshape(8, 1024), ffn_in[:, :1024]])
    half_b = jnp.stack([jnp.concatenate([conv_out.T, proj_half], axis=1), ffn_in[:, 1024:]])
    mine = jnp.where(core == 0, half_a, half_b)
    theirs = from_offset(jnp.where(core == 0, half_b, half_a), "c", 1)
    block = jnp.concatenate(
        [jnp.where(core == 0, mine, theirs), jnp.where(core == 0, theirs, mine)], axis=1
    )
    info = jnp.stack(
        [x, y, core, jnp.where(where == 0, PAD, 0),
         jnp.where(where == peers - 1, PAD + ROWS, WITH_HALO), z, jnp.where(core == 0, y, x)]
    ).astype(jnp.int32)

    pieces = spread_z(block, core)
    out_halves = jnp.stack([ffn_out.T[:, :1024], ffn_out.T[:, 1024:]])
    out_halves, _ = lax.optimization_barrier((out_halves, [p[3] for p in pieces[1:3]]))
    out_halves = jnp.broadcast_to(out_halves[:, None], (X, YL, CORE, YH, 8, D))
    out_plane = lax.all_to_all(
        out_halves.reshape(-1, 8, D), ("x", "yl", "c", "yh"), 0, 0, tiled=True
    )

    def plan_z(info_ref):
        steps = []
        for i, (k, _, rows, _) in enumerate(pieces):
            for j in range(abs(rows)):
                at = lax.rem(info_ref[5] + k + (j if rows > 0 else -j), Z)
                steps.append((i, j, 0, (slice(None), at)))
        return steps

    z_blocks, out_plane = lax.optimization_barrier(([p[3] for p in pieces], out_plane))
    out_plane = out_plane.reshape(X, YL, CORE, YH, 8, D).transpose(3, 0, 1, 2, 4, 5)
    out_pieces = [out_plane.reshape(YH, X, YL, 16, D)]

    def more_out(steps):
        for _ in range(steps):
            out_pieces.append(one_way_z(out_pieces[-1]))

    more_out(2)
    (first,) = place(z_blocks, info, plan_z, [(2, Z, 16, D)])
    middle = middle_ring(first)

    def plan_middle(info_ref):
        return [
            (i, half, half, lax.rem(info_ref[6] + k, 4))
            for half in range(2)
            for i, (k, *_) in enumerate(middle)
        ]

    blocks, out_pieces[-1] = lax.optimization_barrier(([p[3] for p in middle], out_pieces[-1]))
    front_block, in_block = place(blocks, info, plan_middle, [(4, Z, 16, D)] * 2)
    front_low, front_high, front_rest = last_ring(front_block)
    frames, front_block = lax.optimization_barrier((frames, front_block))
    pairs = [(i, i ^ 1) for i in range(peers)]
    start, end = frames[:EDGE], frames[-EDGE:]
    near = lax.ppermute(jnp.where(yh == 0, end, start), ALL, pairs)
    pairs = [(i, j) for i in range(peers) if 0 <= (j := i + 2 * (i % 2) - 1) < peers]
    far = lax.ppermute(jnp.where(yh == 0, start, end), ALL, pairs)
    before, after = jnp.where(yh == 0, far, near), jnp.where(yh == 0, near, far)
    reduced = pl.pallas_call(
        reduce_kernel,
        out_shape=jax.ShapeDtypeStruct((WITH_HALO, D), BF16),
        in_specs=[VMEM] * 4,
        out_specs=VMEM,
        scratch_shapes=[pltpu.VMEM((DIN // 128, 2 * EDGE + frames.shape[0], 128), F32)],
        compiler_params=params(12),
        cost_estimate=cost(2 * WITH_HALO * DIN * D, 10**7),
    )(before, frames, after, down)
    more_out(1)
    other_own = from_offset(front_block, "c", 1)
    front_low, front_high, reduced, in_block, out_pieces[-1], other_own = lax.optimization_barrier(
        (front_low, front_high, reduced, in_block, out_pieces[-1], other_own)
    )
    front_pieces = front_rest(front_low, front_high)
    other_next = [from_offset(p[3], "c", 1) for p in front_pieces[1:3]]
    in_low, in_high, in_rest = last_ring(in_block)
    more_out(2)
    in_low, in_high, reduced, out_pieces[-1], other_next = lax.optimization_barrier(
        (in_low, in_high, reduced, out_pieces[-1], other_next)
    )
    in_pieces = in_rest(in_low, in_high)
    more_out(1)
    front_other = [other_own, *other_next, *(from_offset(p, "c", 1) for *_, p in front_pieces[3:])]

    offsets = [p[:3] for p in front_pieces]
    mixed, norm = pl.pallas_call(
        functools.partial(front_kernel, offsets),
        out_shape=(jax.ShapeDtypeStruct((ROWS, D), F32), jax.ShapeDtypeStruct((ROWS, D), BF16)),
        in_specs=[SMEM, VMEM] + [ANY] * (2 * len(offsets)),
        out_specs=(VMEM, VMEM),
        scratch_shapes=[
            pltpu.VMEM((2, YH, X, Z, YL, 16, D), BF16),
            pltpu.VMEM((WITH_HALO, 512), F32),
            pltpu.SemaphoreType.DMA((32,)),
        ],
        compiler_params=params(),
        cost_estimate=cost(2 * WITH_HALO * D * D * 4, 10**7),
    )(info, reduced, *[p[3] for p in front_pieces], *front_other)

    offsets = [p[:3] for p in in_pieces]
    in_pieces = [p[3] for p in in_pieces]
    norm, in_pieces, out_pieces = lax.optimization_barrier((norm, in_pieces, out_pieces))
    more_out(1)
    norm_other = from_offset(norm, "c", 1)
    whole = pltpu.VMEM((YH, X, Z, YL, 16, D), BF16)
    hidden, share = pl.pallas_call(
        functools.partial(other_kernel, offsets),
        out_shape=(
            jax.ShapeDtypeStruct((YH, ROWS, D), BF16),
            jax.ShapeDtypeStruct((ROWS, D), BF16),
        ),
        in_specs=[SMEM, VMEM, VMEM] + [ANY] * (len(offsets) + Z),
        out_specs=(VMEM, VMEM),
        scratch_shapes=[
            whole, whole, pltpu.SemaphoreType.DMA((16,)), pltpu.SemaphoreType.DMA((Z,))
        ],
        compiler_params=params(),
        cost_estimate=cost(6 * 2 * ROWS * D * D, 10**7),
    )(info, norm, norm_other, *in_pieces, *out_pieces)
    share = from_offset(share, "c", 1)
    own = pl.pallas_call(
        own_kernel,
        out_shape=jax.ShapeDtypeStruct((ROWS, D), F32),
        in_specs=[SMEM, VMEM, VMEM] + [ANY] * Z,
        out_specs=VMEM,
        scratch_shapes=[whole, pltpu.SemaphoreType.DMA((Z,))],
        compiler_params=params(),
        cost_estimate=cost(2 * 2 * ROWS * D * D, 10**7),
    )(info, hidden, mixed, *out_pieces)
    return (own + 0.5 * share.astype(F32)).astype(BF16)


def solution(mesh):
    parts = Mesh(mesh.devices.reshape(X, Z, YL, CORE, YH), ALL)
    return jax.shard_map(
        body,
        mesh=parts,
        in_specs=(
            P(ALL, None),
            P(),
            P(WIDE, None),
            P(WIDE, None, "yh"),
            P(None, "yh"),
            P("yh", WIDE),
            P(WIDE, "yh"),
            P("yh", WIDE),
        ),
        out_specs=P(ALL, None),
        check_vma=False,
    )
```

```python
import functools
import itertools

import jax
import jax.numpy as jnp
from jax import lax
from jax.experimental import pallas as pl
from jax.experimental.pallas import tpu as pltpu
from jax.sharding import Mesh
from jax.sharding import PartitionSpec as P

X, Z, YL, CORE, YH = 4, 8, 2, 2, 2
ALL = ("x", "z", "yl", "c", "yh")
WIDE = ("x", "z", "yl", "c")
Y = ("yl", "yh")
TAPS, REACH, PAD = 15, 7, 8
ROWS, DIN, D = 256, 768, 1024
WITH_HALO = ROWS + 2 * PAD
EDGE = 32
BF16, F32 = jnp.bfloat16, jnp.float32
ANY = pl.BlockSpec(memory_space=pl.ANY)
VMEM = pl.BlockSpec(memory_space=pltpu.VMEM)
SMEM = pl.BlockSpec(memory_space=pltpu.SMEM)


def params(mib=20):
    return pltpu.CompilerParams(vmem_limit_bytes=mib * 2**20)


def cost(flops, moved):
    return pl.CostEstimate(flops=flops, bytes_accessed=moved, transcendentals=0)


def from_offset(block, axis, offset):
    peers = lax.axis_size(axis)
    index = [0, 2, 1, 3] if axis == Y else range(peers)
    pairs = [(index[j], index[(j - offset) % peers]) for j in range(peers)]
    return lax.ppermute(block, axis, pairs)


def crossed(block, offset, x_core):
    pairs = []
    for x, y, core in itertools.product(range(X), range(YL * YH), range(CORE)):
        to = ((x - offset) % X, y) if core == x_core else (x, (y - offset) % (YL * YH))
        index = [((i * YL + j % YL) * CORE + core) * YH + j // YL for i, j in ((x, y), to)]
        pairs.append(tuple(index))
    return lax.ppermute(block, ("x", "yl", "c", "yh"), pairs)


def middle_ring(block):
    after, before = crossed(block, 1, 1), crossed(block, -1, 1)
    full = block.shape[0]
    return [(0, 0, full, block), (1, 0, full, after), (3, 0, full, before),
            (2, 0, full, crossed(after, 1, 1))]


def last_ring(block):
    half, full = block.shape[0] // 2, block.shape[0]
    after, before = crossed(block, 1, 0), crossed(block, -1, 0)

    def rest(low, high):
        low, high = crossed(low, 1, 0), crossed(high, -1, 0)
        return [(0, 0, full, block), (1, 0, full, after), (3, 0, full, before),
                (2, 0, half, low), (2, half, half, high)]

    return after[:half], before[half:], rest


def one_way_z(block, up_core=0):
    pairs = []
    for z, core in itertools.product(range(Z), range(CORE)):
        to = (z - 1) % Z if core == up_core else (z + 1) % Z
        pairs.append((z * CORE + core, to * CORE + core))
    return lax.ppermute(block, ("z", "c"), pairs)


def spread_z(block, core):
    after, before = from_offset(block, "z", 1), from_offset(block, "z", -1)
    two_after = from_offset(jnp.stack([block, after]), "z", 2)
    two_before = from_offset(jnp.stack([block, before]), "z", -2)
    pairs = []
    for z, c in itertools.product(range(Z), range(CORE)):
        to = (z - 3) % Z if c == 0 else (z + 3) % Z
        pairs.append((z * CORE + c, to * CORE + c))
    far = lax.ppermute(jnp.where(core == 0, after, before), ("z", "c"), pairs)
    return [(0, 0, 1, block[None]), (1, 0, 1, after[None]), (7, 0, 1, before[None]),
            (2, 0, 2, two_after), (6, 0, -2, two_before), (4, 0, 1, far[None])]


def place(pieces, info, plan, out_shapes):
    count = len(plan([0] * info.shape[0]))

    def kernel(info_ref, *refs):
        ins, outs, sems = refs[: len(pieces)], refs[len(pieces) : -1], refs[-1]
        copies = []
        for i, (piece, part, out, at) in enumerate(plan(info_ref)):
            source = ins[piece] if part is None else ins[piece].at[part]
            copies.append(pltpu.make_async_copy(source, outs[out].at[at], sems.at[i]))
        for copy in copies:
            copy.start()
        for copy in copies:
            copy.wait()

    moved = 2 * sum(2 * b.size for b in pieces)
    return pl.pallas_call(
        kernel,
        out_shape=[jax.ShapeDtypeStruct(s, BF16) for s in out_shapes],
        in_specs=[SMEM] + [ANY] * len(pieces),
        out_specs=[ANY] * len(out_shapes),
        scratch_shapes=[pltpu.SemaphoreType.DMA((count,))],
        compiler_params=params(4),
        cost_estimate=cost(0, moved),
    )(info, *pieces)


def layer_norm(values):
    centre = jnp.mean(values, axis=-1, keepdims=True)
    centred = values - centre
    spread = jnp.mean(centred * centred, axis=-1, keepdims=True)
    return centred * lax.rsqrt(spread + 1e-05)


def reduce_kernel(before_ref, frames_ref, after_ref, taps_ref, out_ref, wide):
    rows = frames_ref.shape[0]
    columns = []
    for j in range(DIN // 128):
        lanes = slice(j * 128, (j + 1) * 128)
        wide[j, 0:EDGE] = before_ref[:, lanes].astype(F32)
        wide[j, EDGE : EDGE + rows] = frames_ref[:, lanes].astype(F32)
        wide[j, EDGE + rows :] = after_ref[:, lanes].astype(F32)
        total = jnp.zeros((WITH_HALO, 128), F32)
        for k in range(TAPS):
            start = EDGE - 2 * PAD - REACH + k
            window = wide[j, pl.ds(start, WITH_HALO, stride=2), :]
            total = total + taps_ref[k : k + 1, lanes].astype(F32) * window
        columns.append(total.astype(BF16))
    reduced = jnp.concatenate(columns, axis=1)
    lane = lax.broadcasted_iota(jnp.int32, (DIN, D), 1)
    row = lax.broadcasted_iota(jnp.int32, (DIN, D), 0)
    source = (lane >> 3) * 6 + (lane & 7)
    spread = jnp.where((source == row) & ((lane & 7) < 6), 1.0, 0.0).astype(BF16)
    out_ref[...] = jnp.dot(reduced, spread, preferred_element_type=F32).astype(BF16)


def dot_t(a, b):
    return lax.dot_general(a, b, (((1,), (1,)), ((), ())), preferred_element_type=F32)


def start_copies(pairs, sems):
    copies = [
        pltpu.make_async_copy(source, target, sems.at[i])
        for i, (source, target) in enumerate(pairs)
    ]
    for copy in copies:
        copy.start()
    return copies


def crossed_copies(refs, offsets, weights, x, y, core):
    pairs = []
    last = jnp.where(core == 0, x, y)
    for ref, (k, start, rows) in zip(refs, offsets, strict=True):
        at = lax.rem(last + k, 4)
        for m in range(rows):
            to_x = jnp.where(core == 0, at, start + m)
            to_y = jnp.where(core == 0, start + m, at)
            pairs.append((ref.at[m], weights.at[to_y // YL, to_x, :, lax.rem(to_y, YL)]))
    return pairs


def front_kernel(offsets, info_ref, reduced_ref, *refs):
    n = len(offsets)
    own, other = refs[:n], refs[n : 2 * n]
    mixed_ref, norm_ref, weights, gated_ref, sems = refs[2 * n :]
    x, y, core = info_ref[0], info_ref[1], info_ref[2]
    own_pairs = crossed_copies(own, offsets, weights.at[core], x, y, core)
    start_copies(own_pairs, sems.at[core])
    start_copies(crossed_copies(other, offsets, weights.at[1 - core], x, y, 1 - core), sems.at[1 - core])

    def wait_side(side):
        for i, (source, target) in enumerate(own_pairs):
            pltpu.make_async_copy(source, target, sems.at[side, i]).wait()

    wait_side(1)

    def mat(side, yh):
        return weights[side, yh].reshape(D, D)

    reduced = reduced_ref[...]
    projected = jnp.concatenate(
        [jnp.dot(reduced, mat(1, yh)[:, 512:], preferred_element_type=F32).astype(BF16) for yh in range(YH)], axis=1)
    projected = projected.astype(F32)
    normed = layer_norm(projected).astype(BF16)
    row = lax.broadcasted_iota(jnp.int32, (WITH_HALO, 1), 0)
    inside = (row >= info_ref[3]) & (row < info_ref[4])
    mixed = projected[PAD : PAD + ROWS]
    wait_side(0)
    for yh in range(YH):
        pre = jnp.dot(normed, mat(0, yh), preferred_element_type=F32)
        gated = (pre[:, :512] * jax.nn.sigmoid(pre[:, 512:])).astype(BF16).astype(F32)
        gated_ref[...] = jnp.where(inside, gated, 0.0)
        depth = jnp.zeros((ROWS, 512), F32)
        for k in range(TAPS):
            tap_rows = weights[1, yh, 0, k // 8, (k // 4) % 2][:, 512:].astype(F32)
            at = 8 * ((k // 2) % 2) + 6 + k % 2
            tap = tap_rows[at : at + 1]
            depth = depth + tap * gated_ref[pl.ds(PAD - REACH + k, ROWS), :]
        activated = jax.nn.silu(depth).astype(BF16)
        mixed = mixed + dot_t(activated, mat(1, yh)[:, :512])
    mixed_ref[...] = mixed
    norm_ref[...] = layer_norm(mixed).astype(BF16)


def hidden_of(rows, weights, yh):
    pre = jnp.dot(rows, weights[yh].reshape(D, D), preferred_element_type=F32)
    return jax.nn.silu(pre).astype(BF16)


def out_copies(refs, weights, z, core, sems):
    pairs = []
    for k, ref in enumerate(refs):
        at = lax.rem(z + jnp.where(core == 0, k, Z - k), Z)
        pairs.append((ref, weights.at[:, :, at]))
    return start_copies(pairs, sems)


def other_kernel(offsets, info_ref, own_ref, other_ref, *refs):
    n = len(offsets)
    pieces, out_pieces = refs[:n], refs[n : n + Z]
    hidden_ref, share_ref, first, second, sems, out_sems = refs[n + Z :]
    pairs = crossed_copies(pieces, offsets, first, info_ref[0], info_ref[1], info_ref[2])
    copies = start_copies(pairs, sems)
    later = out_copies(out_pieces, second, info_ref[5], info_ref[2], out_sems)
    for copy in copies:
        copy.wait()
    hidden = [hidden_of(other_ref[...], first, yh) for yh in range(YH)]
    for yh in range(YH):
        hidden_ref[yh] = hidden_of(own_ref[...], first, yh)
    for copy in later:
        copy.wait()
    total = dot_t(hidden[0], second[0].reshape(D, D))
    share_ref[...] = (total + dot_t(hidden[1], second[1].reshape(D, D))).astype(BF16)


def own_kernel(info_ref, hidden_ref, mixed_ref, *refs):
    out_pieces, (out_ref, second, out_sems) = refs[:Z], refs[Z:]
    for copy in out_copies(out_pieces, second, info_ref[5], info_ref[2], out_sems):
        copy.wait()
    total = dot_t(hidden_ref[0], second[0].reshape(D, D))
    total = total + dot_t(hidden_ref[1], second[1].reshape(D, D))
    out_ref[...] = mixed_ref[...] + 0.5 * total


def body(frames, down, proj, glu, conv_taps, conv_out, ffn_in, ffn_out):
    core, x, z = lax.axis_index("c"), lax.axis_index("x"), lax.axis_index("z")
    yh, yl = lax.axis_index("yh"), lax.axis_index("yl")
    y = yh * YL + yl
    where = lax.axis_index(ALL)
    peers = lax.axis_size(ALL)

    proj_half = lax.dynamic_slice_in_dim(proj, yh * 512, 512, 1)
    taps_at = 2 * (lax.rem(z, 2) * 4 + yl * 2 + core)
    taps = lax.dynamic_slice_in_dim(jnp.pad(conv_taps, ((0, 1), (0, 0))), taps_at, 2, 0)
    proj_half = jnp.concatenate([proj_half, taps], axis=0)
    half_a = jnp.stack([glu.reshape(8, 1024), ffn_in[:, :1024]])
    half_b = jnp.stack([jnp.concatenate([conv_out.T, proj_half], axis=1), ffn_in[:, 1024:]])
    mine = jnp.where(core == 0, half_a, half_b)
    theirs = from_offset(jnp.where(core == 0, half_b, half_a), "c", 1)
    out_halves = jnp.stack([ffn_out.T[:, :1024], ffn_out.T[:, 1024:]])
    out_halves = jnp.broadcast_to(out_halves[:, None], (X, YL, CORE, YH, 8, D))
    out_plane = lax.all_to_all(
        out_halves.reshape(-1, 8, D), ("x", "yl", "c", "yh"), 0, 0, tiled=True
    )
    block = jnp.concatenate(
        [jnp.where(core == 0, mine, theirs), jnp.where(core == 0, theirs, mine)], axis=1
    )
    info = jnp.stack(
        [x, y, core, jnp.where(where == 0, PAD, 0),
         jnp.where(where == peers - 1, PAD + ROWS, WITH_HALO), z, jnp.where(core == 0, y, x)]
    ).astype(jnp.int32)

    pieces = spread_z(block, core)

    def plan_z(info_ref):
        steps = []
        for i, (k, _, rows, _) in enumerate(pieces):
            for j in range(abs(rows)):
                at = lax.rem(info_ref[5] + k + (j if rows > 0 else -j), Z)
                steps.append((i, j, 0, (slice(None), at)))
        return steps

    z_blocks, out_plane = lax.optimization_barrier(([p[3] for p in pieces], out_plane))
    out_plane = out_plane.reshape(X, YL, CORE, YH, 8, D).transpose(3, 0, 1, 2, 4, 5)
    out_pieces = [out_plane.reshape(YH, X, YL, 16, D)]

    def more_out(steps):
        for _ in range(steps):
            out_pieces.append(one_way_z(out_pieces[-1]))

    more_out(2)
    (first,) = place(z_blocks, info, plan_z, [(2, Z, 16, D)])
    middle = middle_ring(first)

    def plan_middle(info_ref):
        return [
            (i, half, half, lax.rem(info_ref[6] + k, 4))
            for half in range(2)
            for i, (k, *_) in enumerate(middle)
        ]

    frames, first = lax.optimization_barrier((frames, first))
    pairs = [(i, i ^ 1) for i in range(peers)]
    start, end = frames[:EDGE], frames[-EDGE:]
    near = lax.ppermute(jnp.where(yh == 0, end, start), ALL, pairs)
    pairs = [(i, j) for i in range(peers) if 0 <= (j := i + 2 * (i % 2) - 1) < peers]
    far = lax.ppermute(jnp.where(yh == 0, start, end), ALL, pairs)
    before, after = jnp.where(yh == 0, far, near), jnp.where(yh == 0, near, far)
    blocks, out_pieces[-1], before, after = lax.optimization_barrier(
        ([p[3] for p in middle], out_pieces[-1], before, after)
    )
    front_block, in_block = place(blocks, info, plan_middle, [(4, Z, 16, D)] * 2)
    front_low, front_high, front_rest = last_ring(front_block)
    other_own = from_offset(front_block, "c", 1)
    in_block, other_own = lax.optimization_barrier((in_block, other_own))
    in_low, in_high, in_rest = last_ring(in_block)
    reduced = pl.pallas_call(
        reduce_kernel,
        out_shape=jax.ShapeDtypeStruct((WITH_HALO, D), BF16),
        in_specs=[VMEM] * 4,
        out_specs=VMEM,
        scratch_shapes=[pltpu.VMEM((DIN // 128, 2 * EDGE + frames.shape[0], 128), F32)],
        compiler_params=params(12),
        cost_estimate=cost(2 * WITH_HALO * DIN * D, 10**7),
    )(before, frames, after, down)
    more_out(1)
    out_pieces[-1], reduced = lax.optimization_barrier((out_pieces[-1], reduced))
    more_out(1)
    front_low, front_high, out_pieces[-1] = lax.optimization_barrier(
        (front_low, front_high, out_pieces[-1])
    )
    front_pieces = front_rest(front_low, front_high)
    more_out(1)
    in_low, in_high, out_pieces[-1], next_blocks = lax.optimization_barrier(
        (in_low, in_high, out_pieces[-1], [p[3] for p in front_pieces[1:3]])
    )
    front_other = [other_own] + [from_offset(block, "c", 1) for block in next_blocks]
    in_low, in_high, _ = lax.optimization_barrier(
        (in_low, in_high, [p[3] for p in front_pieces[3:]])
    )
    in_pieces = in_rest(in_low, in_high)
    more_out(1)
    out_first, _ = lax.optimization_barrier((out_pieces[0], out_pieces[4]))
    out_pieces.append(one_way_z(out_first, up_core=1))
    front_other += [from_offset(p, "c", 1) for *_, p in front_pieces[3:]]

    offsets = [p[:3] for p in front_pieces]
    mixed, norm = pl.pallas_call(
        functools.partial(front_kernel, offsets),
        out_shape=(jax.ShapeDtypeStruct((ROWS, D), F32), jax.ShapeDtypeStruct((ROWS, D), BF16)),
        in_specs=[SMEM, VMEM] + [ANY] * (2 * len(offsets)),
        out_specs=(VMEM, VMEM),
        scratch_shapes=[
            pltpu.VMEM((2, YH, X, Z, YL, 16, D), BF16),
            pltpu.VMEM((WITH_HALO, 512), F32),
            pltpu.SemaphoreType.DMA((2, 16)),
        ],
        compiler_params=params(),
        cost_estimate=cost(2 * WITH_HALO * D * D * 4, 10**7),
    )(info, reduced, *[p[3] for p in front_pieces], *front_other)

    offsets = [p[:3] for p in in_pieces]
    in_pieces = [p[3] for p in in_pieces]
    norm, in_pieces, out_pieces[7] = lax.optimization_barrier((norm, in_pieces, out_pieces[7]))
    norm_other = from_offset(norm, "c", 1)
    whole = pltpu.VMEM((YH, X, Z, YL, 16, D), BF16)
    hidden, share = pl.pallas_call(
        functools.partial(other_kernel, offsets),
        out_shape=(
            jax.ShapeDtypeStruct((YH, ROWS, D), BF16),
            jax.ShapeDtypeStruct((ROWS, D), BF16),
        ),
        in_specs=[SMEM, VMEM, VMEM] + [ANY] * (len(offsets) + Z),
        out_specs=(VMEM, VMEM),
        scratch_shapes=[
            whole, whole, pltpu.SemaphoreType.DMA((16,)), pltpu.SemaphoreType.DMA((Z,))
        ],
        compiler_params=params(),
        cost_estimate=cost(6 * 2 * ROWS * D * D, 10**7),
    )(info, norm, norm_other, *in_pieces, *out_pieces)
    share = from_offset(share, "c", 1)
    own = pl.pallas_call(
        own_kernel,
        out_shape=jax.ShapeDtypeStruct((ROWS, D), F32),
        in_specs=[SMEM, VMEM, VMEM] + [ANY] * Z,
        out_specs=VMEM,
        scratch_shapes=[whole, pltpu.SemaphoreType.DMA((Z,))],
        compiler_params=params(),
        cost_estimate=cost(2 * 2 * ROWS * D * D, 10**7),
    )(info, hidden, mixed, *out_pieces)
    return (own + 0.5 * share.astype(F32)).astype(BF16)


def solution(mesh):
    parts = Mesh(mesh.devices.reshape(X, Z, YL, CORE, YH), ALL)
    return jax.shard_map(
        body,
        mesh=parts,
        in_specs=(
            P(ALL, None),
            P(),
            P(WIDE, None),
            P(WIDE, None, "yh"),
            P(None, "yh"),
            P("yh", WIDE),
            P(WIDE, "yh"),
            P("yh", WIDE),
        ),
        out_specs=P(ALL, None),
        check_vma=False,
    )
```

```python
import functools
import itertools

import jax
import jax.numpy as jnp
from jax import lax
from jax.experimental import pallas as pl
from jax.experimental.pallas import tpu as pltpu
from jax.sharding import Mesh
from jax.sharding import PartitionSpec as P

X, Z, YL, CORE, YH = 4, 8, 2, 2, 2
ALL = ("x", "z", "yl", "c", "yh")
WIDE = ("x", "z", "yl", "c")
Y = ("yl", "yh")
TAPS, REACH, PAD = 15, 7, 8
ROWS, DIN, D = 256, 768, 1024
WITH_HALO = ROWS + 2 * PAD
EDGE = 32
BF16, F32 = jnp.bfloat16, jnp.float32
ANY = pl.BlockSpec(memory_space=pl.ANY)
VMEM = pl.BlockSpec(memory_space=pltpu.VMEM)
SMEM = pl.BlockSpec(memory_space=pltpu.SMEM)


def params(mib=20):
    return pltpu.CompilerParams(vmem_limit_bytes=mib * 2**20)


def cost(flops, moved):
    return pl.CostEstimate(flops=flops, bytes_accessed=moved, transcendentals=0)


def from_offset(block, axis, offset):
    peers = lax.axis_size(axis)
    index = [0, 2, 1, 3] if axis == Y else range(peers)
    pairs = [(index[j], index[(j - offset) % peers]) for j in range(peers)]
    return lax.ppermute(block, axis, pairs)


def crossed(block, offset, x_core):
    pairs = []
    for x, y, core in itertools.product(range(X), range(YL * YH), range(CORE)):
        to = ((x - offset) % X, y) if core == x_core else (x, (y - offset) % (YL * YH))
        index = [((i * YL + j % YL) * CORE + core) * YH + j // YL for i, j in ((x, y), to)]
        pairs.append(tuple(index))
    return lax.ppermute(block, ("x", "yl", "c", "yh"), pairs)


def middle_ring(block):
    after, before = crossed(block, 1, 1), crossed(block, -1, 1)
    full = block.shape[0]
    return [(0, 0, full, block), (1, 0, full, after), (3, 0, full, before),
            (2, 0, full, crossed(after, 1, 1))]


def last_ring(block):
    half, full = block.shape[0] // 2, block.shape[0]
    after, before = crossed(block, 1, 0), crossed(block, -1, 0)

    def rest(low, high):
        low, high = crossed(low, 1, 0), crossed(high, -1, 0)
        return [(0, 0, full, block), (1, 0, full, after), (3, 0, full, before),
                (2, 0, half, low), (2, half, half, high)]

    return after[:half], before[half:], rest


def one_way_z(block, up_core=0):
    pairs = []
    for z, core in itertools.product(range(Z), range(CORE)):
        to = (z - 1) % Z if core == up_core else (z + 1) % Z
        pairs.append((z * CORE + core, to * CORE + core))
    return lax.ppermute(block, ("z", "c"), pairs)


def spread_z(block, core):
    after, before = from_offset(block, "z", 1), from_offset(block, "z", -1)
    two_after = from_offset(jnp.stack([block, after]), "z", 2)
    two_before = from_offset(jnp.stack([block, before]), "z", -2)
    pairs = []
    for z, c in itertools.product(range(Z), range(CORE)):
        to = (z - 3) % Z if c == 0 else (z + 3) % Z
        pairs.append((z * CORE + c, to * CORE + c))
    far = lax.ppermute(jnp.where(core == 0, after, before), ("z", "c"), pairs)
    return [(0, 0, 1, block[None]), (1, 0, 1, after[None]), (7, 0, 1, before[None]),
            (2, 0, 2, two_after), (6, 0, -2, two_before), (4, 0, 1, far[None])]


def place(pieces, info, plan, out_shapes):
    count = len(plan([0] * info.shape[0]))

    def kernel(info_ref, *refs):
        ins, outs, sems = refs[: len(pieces)], refs[len(pieces) : -1], refs[-1]
        copies = []
        for i, (piece, part, out, at) in enumerate(plan(info_ref)):
            source = ins[piece] if part is None else ins[piece].at[part]
            copies.append(pltpu.make_async_copy(source, outs[out].at[at], sems.at[i]))
        for copy in copies:
            copy.start()
        for copy in copies:
            copy.wait()

    moved = 2 * sum(2 * b.size for b in pieces)
    return pl.pallas_call(
        kernel,
        out_shape=[jax.ShapeDtypeStruct(s, BF16) for s in out_shapes],
        in_specs=[SMEM] + [ANY] * len(pieces),
        out_specs=[ANY] * len(out_shapes),
        scratch_shapes=[pltpu.SemaphoreType.DMA((count,))],
        compiler_params=params(4),
        cost_estimate=cost(0, moved),
    )(info, *pieces)


def layer_norm(values):
    centre = jnp.mean(values, axis=-1, keepdims=True)
    centred = values - centre
    spread = jnp.mean(centred * centred, axis=-1, keepdims=True)
    return centred * lax.rsqrt(spread + 1e-05)


def reduce_kernel(before_ref, frames_ref, after_ref, taps_ref, out_ref, wide):
    rows = frames_ref.shape[0]
    columns = []
    for j in range(DIN // 128):
        lanes = slice(j * 128, (j + 1) * 128)
        wide[j, 0:EDGE] = before_ref[:, lanes].astype(F32)
        wide[j, EDGE : EDGE + rows] = frames_ref[:, lanes].astype(F32)
        wide[j, EDGE + rows :] = after_ref[:, lanes].astype(F32)
        total = jnp.zeros((WITH_HALO, 128), F32)
        for k in range(TAPS):
            start = EDGE - 2 * PAD - REACH + k
            window = wide[j, pl.ds(start, WITH_HALO, stride=2), :]
            total = total + taps_ref[k : k + 1, lanes].astype(F32) * window
        columns.append(total.astype(BF16))
    reduced = jnp.concatenate(columns, axis=1)
    lane = lax.broadcasted_iota(jnp.int32, (DIN, D), 1)
    row = lax.broadcasted_iota(jnp.int32, (DIN, D), 0)
    source = (lane >> 3) * 6 + (lane & 7)
    spread = jnp.where((source == row) & ((lane & 7) < 6), 1.0, 0.0).astype(BF16)
    out_ref[...] = jnp.dot(reduced, spread, preferred_element_type=F32).astype(BF16)


def dot_t(a, b):
    return lax.dot_general(a, b, (((1,), (1,)), ((), ())), preferred_element_type=F32)


def start_copies(pairs, sems):
    copies = [
        pltpu.make_async_copy(source, target, sems.at[i])
        for i, (source, target) in enumerate(pairs)
    ]
    for copy in copies:
        copy.start()
    return copies


def crossed_copies(refs, offsets, weights, x, y, core):
    pairs = []
    last = jnp.where(core == 0, x, y)
    for ref, (k, start, rows) in zip(refs, offsets, strict=True):
        at = lax.rem(last + k, 4)
        for m in range(rows):
            to_x = jnp.where(core == 0, at, start + m)
            to_y = jnp.where(core == 0, start + m, at)
            pairs.append((ref.at[m], weights.at[to_y // YL, to_x, :, lax.rem(to_y, YL)]))
    return pairs


def front_kernel(offsets, info_ref, reduced_ref, *refs):
    n = len(offsets)
    own, other = refs[:n], refs[n : 2 * n]
    mixed_ref, norm_ref, weights, gated_ref, sems = refs[2 * n :]
    x, y, core = info_ref[0], info_ref[1], info_ref[2]
    own_pairs = crossed_copies(own, offsets, weights.at[core], x, y, core)
    start_copies(own_pairs, sems.at[core])
    start_copies(crossed_copies(other, offsets, weights.at[1 - core], x, y, 1 - core), sems.at[1 - core])

    def wait_side(side):
        for i, (source, target) in enumerate(own_pairs):
            pltpu.make_async_copy(source, target, sems.at[side, i]).wait()

    wait_side(1)

    def mat(side, yh):
        return weights[side, yh].reshape(D, D)

    reduced = reduced_ref[...]
    projected = jnp.concatenate(
        [jnp.dot(reduced, mat(1, yh)[:, 512:], preferred_element_type=F32).astype(BF16) for yh in range(YH)], axis=1)
    projected = projected.astype(F32)
    normed = layer_norm(projected).astype(BF16)
    row = lax.broadcasted_iota(jnp.int32, (WITH_HALO, 1), 0)
    inside = (row >= info_ref[3]) & (row < info_ref[4])
    mixed = projected[PAD : PAD + ROWS]
    wait_side(0)
    for yh in range(YH):
        pre = jnp.dot(normed, mat(0, yh), preferred_element_type=F32)
        gated = (pre[:, :512] * jax.nn.sigmoid(pre[:, 512:])).astype(BF16).astype(F32)
        gated_ref[...] = jnp.where(inside, gated, 0.0)
        depth = jnp.zeros((ROWS, 512), F32)
        for k in range(TAPS):
            tap_rows = weights[1, yh, 0, k // 8, (k // 4) % 2][:, 512:].astype(F32)
            at = 8 * ((k // 2) % 2) + 6 + k % 2
            tap = tap_rows[at : at + 1]
            depth = depth + tap * gated_ref[pl.ds(PAD - REACH + k, ROWS), :]
        activated = jax.nn.silu(depth).astype(BF16)
        mixed = mixed + dot_t(activated, mat(1, yh)[:, :512])
    mixed_ref[...] = mixed
    norm_ref[...] = layer_norm(mixed).astype(BF16)


def hidden_of(rows, weights, yh):
    pre = jnp.dot(rows, weights[yh].reshape(D, D), preferred_element_type=F32)
    return jax.nn.silu(pre).astype(BF16)


def out_copies(refs, weights, z, core, sems):
    pairs = []
    for k, ref in enumerate(refs):
        at = lax.rem(z + jnp.where(core == 0, k, Z - k), Z)
        pairs.append((ref, weights.at[:, :, at]))
    return start_copies(pairs, sems)


def other_kernel(offsets, info_ref, other_ref, *refs):
    n = len(offsets)
    pieces, out_pieces = refs[:n], refs[n : n + Z]
    share_ref, first, second, sems, out_sems = refs[n + Z :]
    pairs = crossed_copies(pieces, offsets, first, info_ref[0], info_ref[1], info_ref[2])
    copies = start_copies(pairs, sems)
    later = out_copies(out_pieces, second, info_ref[5], info_ref[2], out_sems)
    for copy in copies:
        copy.wait()
    hidden = [hidden_of(other_ref[...], first, yh) for yh in range(YH)]
    for copy in later:
        copy.wait()
    total = dot_t(hidden[0], second[0].reshape(D, D))
    share_ref[...] = (total + dot_t(hidden[1], second[1].reshape(D, D))).astype(BF16)


def hidden_kernel(offsets, info_ref, own_ref, *refs):
    n = len(offsets)
    pieces, (hidden_ref, weights, sems) = refs[:n], refs[n:]
    pairs = crossed_copies(pieces, offsets, weights, info_ref[0], info_ref[1], info_ref[2])
    for copy in start_copies(pairs, sems):
        copy.wait()
    for yh in range(YH):
        hidden_ref[yh] = hidden_of(own_ref[...], weights, yh)


def own_kernel(info_ref, hidden_ref, mixed_ref, *refs):
    out_pieces, (out_ref, second, out_sems) = refs[:Z], refs[Z:]
    for copy in out_copies(out_pieces, second, info_ref[5], info_ref[2], out_sems):
        copy.wait()
    total = dot_t(hidden_ref[0], second[0].reshape(D, D))
    total = total + dot_t(hidden_ref[1], second[1].reshape(D, D))
    out_ref[...] = mixed_ref[...] + 0.5 * total


def body(frames, down, proj, glu, conv_taps, conv_out, ffn_in, ffn_out):
    core, x, z = lax.axis_index("c"), lax.axis_index("x"), lax.axis_index("z")
    yh, yl = lax.axis_index("yh"), lax.axis_index("yl")
    y = yh * YL + yl
    where = lax.axis_index(ALL)
    peers = lax.axis_size(ALL)

    proj_half = lax.dynamic_slice_in_dim(proj, yh * 512, 512, 1)
    taps_at = 2 * (lax.rem(z, 2) * 4 + yl * 2 + core)
    taps = lax.dynamic_slice_in_dim(jnp.pad(conv_taps, ((0, 1), (0, 0))), taps_at, 2, 0)
    proj_half = jnp.concatenate([proj_half, taps], axis=0)
    half_a = jnp.stack([glu.reshape(8, 1024), ffn_in[:, :1024]])
    half_b = jnp.stack([jnp.concatenate([conv_out.T, proj_half], axis=1), ffn_in[:, 1024:]])
    mine = jnp.where(core == 0, half_a, half_b)
    theirs = from_offset(jnp.where(core == 0, half_b, half_a), "c", 1)
    out_halves = jnp.stack([ffn_out.T[:, :1024], ffn_out.T[:, 1024:]])
    out_halves = jnp.broadcast_to(out_halves[:, None], (X, YL, CORE, YH, 8, D))
    out_plane = lax.all_to_all(
        out_halves.reshape(-1, 8, D), ("x", "yl", "c", "yh"), 0, 0, tiled=True
    )
    block = jnp.concatenate(
        [jnp.where(core == 0, mine, theirs), jnp.where(core == 0, theirs, mine)], axis=1
    )
    info = jnp.stack(
        [x, y, core, jnp.where(where == 0, PAD, 0),
         jnp.where(where == peers - 1, PAD + ROWS, WITH_HALO), z, jnp.where(core == 0, y, x)]
    ).astype(jnp.int32)

    pieces = spread_z(block, core)

    def plan_z(info_ref):
        steps = []
        for i, (k, _, rows, _) in enumerate(pieces):
            for j in range(abs(rows)):
                at = lax.rem(info_ref[5] + k + (j if rows > 0 else -j), Z)
                steps.append((i, j, 0, (slice(None), at)))
        return steps

    z_blocks, out_plane = lax.optimization_barrier(([p[3] for p in pieces], out_plane))
    out_plane = out_plane.reshape(X, YL, CORE, YH, 8, D).transpose(3, 0, 1, 2, 4, 5)
    out_pieces = [out_plane.reshape(YH, X, YL, 16, D)]

    def more_out(steps):
        for _ in range(steps):
            out_pieces.append(one_way_z(out_pieces[-1]))

    more_out(2)
    (first,) = place(z_blocks, info, plan_z, [(2, Z, 16, D)])
    middle = middle_ring(first)

    def plan_middle(info_ref):
        return [
            (i, half, half, lax.rem(info_ref[6] + k, 4))
            for half in range(2)
            for i, (k, *_) in enumerate(middle)
        ]

    frames, first = lax.optimization_barrier((frames, first))
    pairs = [(i, i ^ 1) for i in range(peers)]
    start, end = frames[:EDGE], frames[-EDGE:]
    near = lax.ppermute(jnp.where(yh == 0, end, start), ALL, pairs)
    pairs = [(i, j) for i in range(peers) if 0 <= (j := i + 2 * (i % 2) - 1) < peers]
    far = lax.ppermute(jnp.where(yh == 0, start, end), ALL, pairs)
    before, after = jnp.where(yh == 0, far, near), jnp.where(yh == 0, near, far)
    blocks, out_pieces[-1], before, after = lax.optimization_barrier(
        ([p[3] for p in middle], out_pieces[-1], before, after)
    )
    front_block, in_block = place(blocks, info, plan_middle, [(4, Z, 16, D)] * 2)
    front_low, front_high, front_rest = last_ring(front_block)
    other_own = from_offset(front_block, "c", 1)
    reduced = pl.pallas_call(
        reduce_kernel,
        out_shape=jax.ShapeDtypeStruct((WITH_HALO, D), BF16),
        in_specs=[VMEM] * 4,
        out_specs=VMEM,
        scratch_shapes=[pltpu.VMEM((DIN // 128, 2 * EDGE + frames.shape[0], 128), F32)],
        compiler_params=params(12),
        cost_estimate=cost(2 * WITH_HALO * DIN * D, 10**7),
    )(before, frames, after, down)
    more_out(1)
    in_block, reduced = lax.optimization_barrier((in_block, reduced))
    in_low, in_high, in_rest = last_ring(in_block)
    out_pieces[-1], other_own = lax.optimization_barrier((out_pieces[-1], other_own))
    more_out(1)
    front_low, front_high, out_pieces[-1] = lax.optimization_barrier(
        (front_low, front_high, out_pieces[-1])
    )
    front_pieces = front_rest(front_low, front_high)
    more_out(1)
    in_low, in_high, out_pieces[-1], next_blocks = lax.optimization_barrier(
        (in_low, in_high, out_pieces[-1], [p[3] for p in front_pieces[1:3]])
    )
    front_other = [other_own] + [from_offset(block, "c", 1) for block in next_blocks]
    in_low, in_high, _ = lax.optimization_barrier(
        (in_low, in_high, [p[3] for p in front_pieces[3:]])
    )
    in_pieces = in_rest(in_low, in_high)
    more_out(1)
    out_first, _ = lax.optimization_barrier((out_pieces[0], out_pieces[4]))
    out_pieces.append(one_way_z(out_first, up_core=1))
    front_other += [from_offset(p, "c", 1) for *_, p in front_pieces[3:]]

    offsets = [p[:3] for p in front_pieces]
    mixed, norm = pl.pallas_call(
        functools.partial(front_kernel, offsets),
        out_shape=(jax.ShapeDtypeStruct((ROWS, D), F32), jax.ShapeDtypeStruct((ROWS, D), BF16)),
        in_specs=[SMEM, VMEM] + [ANY] * (2 * len(offsets)),
        out_specs=(VMEM, VMEM),
        scratch_shapes=[
            pltpu.VMEM((2, YH, X, Z, YL, 16, D), BF16),
            pltpu.VMEM((WITH_HALO, 512), F32),
            pltpu.SemaphoreType.DMA((2, 16)),
        ],
        compiler_params=params(),
        cost_estimate=cost(2 * WITH_HALO * D * D * 4, 10**7),
    )(info, reduced, *[p[3] for p in front_pieces], *front_other)

    offsets = [p[:3] for p in in_pieces]
    in_pieces = [p[3] for p in in_pieces]
    norm, in_pieces, out_pieces[6:] = lax.optimization_barrier((norm, in_pieces, out_pieces[6:]))
    norm_other = from_offset(norm, "c", 1)
    whole = pltpu.VMEM((YH, X, Z, YL, 16, D), BF16)
    hidden = pl.pallas_call(
        functools.partial(hidden_kernel, offsets),
        out_shape=jax.ShapeDtypeStruct((YH, ROWS, D), BF16),
        in_specs=[SMEM, VMEM] + [ANY] * len(offsets),
        out_specs=VMEM,
        scratch_shapes=[whole, pltpu.SemaphoreType.DMA((16,))],
        compiler_params=params(),
        cost_estimate=cost(2 * 2 * ROWS * D * D, 10**7),
    )(info, norm, *in_pieces)
    norm_other, hidden = lax.optimization_barrier((norm_other, hidden))
    share = pl.pallas_call(
        functools.partial(other_kernel, offsets),
        out_shape=jax.ShapeDtypeStruct((ROWS, D), BF16),
        in_specs=[SMEM, VMEM] + [ANY] * (len(offsets) + Z),
        out_specs=VMEM,
        scratch_shapes=[
            whole, whole, pltpu.SemaphoreType.DMA((16,)), pltpu.SemaphoreType.DMA((Z,))
        ],
        compiler_params=params(),
        cost_estimate=cost(4 * 2 * ROWS * D * D, 10**7),
    )(info, norm_other, *in_pieces, *out_pieces)
    share = from_offset(share, "c", 1)
    own = pl.pallas_call(
        own_kernel,
        out_shape=jax.ShapeDtypeStruct((ROWS, D), F32),
        in_specs=[SMEM, VMEM, VMEM] + [ANY] * Z,
        out_specs=VMEM,
        scratch_shapes=[whole, pltpu.SemaphoreType.DMA((Z,))],
        compiler_params=params(),
        cost_estimate=cost(2 * 2 * ROWS * D * D, 10**7),
    )(info, hidden, mixed, *out_pieces)
    return (own + 0.5 * share.astype(F32)).astype(BF16)


def solution(mesh):
    parts = Mesh(mesh.devices.reshape(X, Z, YL, CORE, YH), ALL)
    return jax.shard_map(
        body,
        mesh=parts,
        in_specs=(
            P(ALL, None),
            P(),
            P(WIDE, None),
            P(WIDE, None, "yh"),
            P(None, "yh"),
            P("yh", WIDE),
            P(WIDE, "yh"),
            P("yh", WIDE),
        ),
        out_specs=P(ALL, None),
        check_vma=False,
    )
```

```python
import functools
import itertools

import jax
import jax.numpy as jnp
from jax import lax
from jax.experimental import pallas as pl
from jax.experimental.pallas import tpu as pltpu
from jax.sharding import Mesh
from jax.sharding import PartitionSpec as P

X, Z, YL, CORE, YH = 4, 8, 2, 2, 2
ALL = ("x", "z", "yl", "c", "yh")
WIDE = ("x", "z", "yl", "c")
Y = ("yl", "yh")
TAPS, REACH, PAD = 15, 7, 8
ROWS, DIN, D = 256, 768, 1024
WITH_HALO = ROWS + 2 * PAD
EDGE = 32
BF16, F32 = jnp.bfloat16, jnp.float32
ANY = pl.BlockSpec(memory_space=pl.ANY)
VMEM = pl.BlockSpec(memory_space=pltpu.VMEM)
SMEM = pl.BlockSpec(memory_space=pltpu.SMEM)


def params(mib=20):
    return pltpu.CompilerParams(vmem_limit_bytes=mib * 2**20)


def cost(flops, moved):
    return pl.CostEstimate(flops=flops, bytes_accessed=moved, transcendentals=0)


def from_offset(block, axis, offset):
    peers = lax.axis_size(axis)
    index = [0, 2, 1, 3] if axis == Y else range(peers)
    pairs = [(index[j], index[(j - offset) % peers]) for j in range(peers)]
    return lax.ppermute(block, axis, pairs)


def crossed(block, offset, x_core):
    pairs = []
    for x, y, core in itertools.product(range(X), range(YL * YH), range(CORE)):
        to = ((x - offset) % X, y) if core == x_core else (x, (y - offset) % (YL * YH))
        index = [((i * YL + j % YL) * CORE + core) * YH + j // YL for i, j in ((x, y), to)]
        pairs.append(tuple(index))
    return lax.ppermute(block, ("x", "yl", "c", "yh"), pairs)


def middle_ring(block):
    after, before = crossed(block, 1, 1), crossed(block, -1, 1)
    full = block.shape[0]
    return [(0, 0, full, block), (1, 0, full, after), (3, 0, full, before),
            (2, 0, full, crossed(after, 1, 1))]


def last_ring(block):
    half, full = block.shape[0] // 2, block.shape[0]
    after, before = crossed(block, 1, 0), crossed(block, -1, 0)

    def rest(low, high):
        low, high = crossed(low, 1, 0), crossed(high, -1, 0)
        return [(0, 0, full, block), (1, 0, full, after), (3, 0, full, before),
                (2, 0, half, low), (2, half, half, high)]

    return after[:half], before[half:], rest


def one_way_z(block, up_core=0):
    pairs = []
    for z, core in itertools.product(range(Z), range(CORE)):
        to = (z - 1) % Z if core == up_core else (z + 1) % Z
        pairs.append((z * CORE + core, to * CORE + core))
    return lax.ppermute(block, ("z", "c"), pairs)


def spread_z(block, core):
    after, before = from_offset(block, "z", 1), from_offset(block, "z", -1)
    two_after = from_offset(jnp.stack([block, after]), "z", 2)
    two_before = from_offset(jnp.stack([block, before]), "z", -2)
    pairs = []
    for z, c in itertools.product(range(Z), range(CORE)):
        to = (z - 3) % Z if c == 0 else (z + 3) % Z
        pairs.append((z * CORE + c, to * CORE + c))
    far = lax.ppermute(jnp.where(core == 0, after, before), ("z", "c"), pairs)
    return [(0, 0, 1, block[None]), (1, 0, 1, after[None]), (7, 0, 1, before[None]),
            (2, 0, 2, two_after), (6, 0, -2, two_before), (4, 0, 1, far[None])]


def place(pieces, info, plan, out_shapes):
    count = len(plan([0] * info.shape[0]))

    def kernel(info_ref, *refs):
        ins, outs, sems = refs[: len(pieces)], refs[len(pieces) : -1], refs[-1]
        copies = []
        for i, (piece, part, out, at) in enumerate(plan(info_ref)):
            source = ins[piece] if part is None else ins[piece].at[part]
            copies.append(pltpu.make_async_copy(source, outs[out].at[at], sems.at[i]))
        for copy in copies:
            copy.start()
        for copy in copies:
            copy.wait()

    moved = 2 * sum(2 * b.size for b in pieces)
    return pl.pallas_call(
        kernel,
        out_shape=[jax.ShapeDtypeStruct(s, BF16) for s in out_shapes],
        in_specs=[SMEM] + [ANY] * len(pieces),
        out_specs=[ANY] * len(out_shapes),
        scratch_shapes=[pltpu.SemaphoreType.DMA((count,))],
        compiler_params=params(4),
        cost_estimate=cost(0, moved),
    )(info, *pieces)


def layer_norm(values):
    centre = jnp.mean(values, axis=-1, keepdims=True)
    centred = values - centre
    spread = jnp.mean(centred * centred, axis=-1, keepdims=True)
    return centred * lax.rsqrt(spread + 1e-05)


def reduce_kernel(before_ref, frames_ref, after_ref, taps_ref, out_ref, wide):
    rows = frames_ref.shape[0]
    columns = []
    for j in range(DIN // 128):
        lanes = slice(j * 128, (j + 1) * 128)
        wide[j, 0:EDGE] = before_ref[:, lanes].astype(F32)
        wide[j, EDGE : EDGE + rows] = frames_ref[:, lanes].astype(F32)
        wide[j, EDGE + rows :] = after_ref[:, lanes].astype(F32)
        total = jnp.zeros((WITH_HALO, 128), F32)
        for k in range(TAPS):
            start = EDGE - 2 * PAD - REACH + k
            window = wide[j, pl.ds(start, WITH_HALO, stride=2), :]
            total = total + taps_ref[k : k + 1, lanes].astype(F32) * window
        columns.append(total.astype(BF16))
    reduced = jnp.concatenate(columns, axis=1)
    lane = lax.broadcasted_iota(jnp.int32, (DIN, D), 1)
    row = lax.broadcasted_iota(jnp.int32, (DIN, D), 0)
    source = (lane >> 3) * 6 + (lane & 7)
    spread = jnp.where((source == row) & ((lane & 7) < 6), 1.0, 0.0).astype(BF16)
    out_ref[...] = jnp.dot(reduced, spread, preferred_element_type=F32).astype(BF16)


def dot_t(a, b):
    return lax.dot_general(a, b, (((1,), (1,)), ((), ())), preferred_element_type=F32)


def start_copies(pairs, sems):
    copies = [
        pltpu.make_async_copy(source, target, sems.at[i])
        for i, (source, target) in enumerate(pairs)
    ]
    for copy in copies:
        copy.start()
    return copies


def crossed_copies(refs, offsets, weights, x, y, core):
    pairs = []
    last = jnp.where(core == 0, x, y)
    for ref, (k, start, rows) in zip(refs, offsets, strict=True):
        at = lax.rem(last + k, 4)
        for m in range(rows):
            to_x = jnp.where(core == 0, at, start + m)
            to_y = jnp.where(core == 0, start + m, at)
            pairs.append((ref.at[m], weights.at[to_y // YL, to_x, :, lax.rem(to_y, YL)]))
    return pairs


def front_kernel(offsets, info_ref, reduced_ref, *refs):
    n = len(offsets)
    own, other = refs[:n], refs[n : 2 * n]
    mixed_ref, norm_ref, weights, gated_ref, sems = refs[2 * n :]
    x, y, core = info_ref[0], info_ref[1], info_ref[2]
    own_pairs = crossed_copies(own, offsets, weights.at[core], x, y, core)
    start_copies(own_pairs, sems.at[core])
    start_copies(crossed_copies(other, offsets, weights.at[1 - core], x, y, 1 - core), sems.at[1 - core])

    def wait_side(side):
        for i, (source, target) in enumerate(own_pairs):
            pltpu.make_async_copy(source, target, sems.at[side, i]).wait()

    wait_side(1)

    def mat(side, yh):
        return weights[side, yh].reshape(D, D)

    reduced = reduced_ref[...]
    projected = jnp.concatenate(
        [jnp.dot(reduced, mat(1, yh)[:, 512:], preferred_element_type=F32).astype(BF16) for yh in range(YH)], axis=1)
    projected = projected.astype(F32)
    normed = layer_norm(projected).astype(BF16)
    row = lax.broadcasted_iota(jnp.int32, (WITH_HALO, 1), 0)
    inside = (row >= info_ref[3]) & (row < info_ref[4])
    mixed = projected[PAD : PAD + ROWS]
    wait_side(0)
    for yh in range(YH):
        pre = jnp.dot(normed, mat(0, yh), preferred_element_type=F32)
        gated = (pre[:, :512] * jax.nn.sigmoid(pre[:, 512:])).astype(BF16).astype(F32)
        gated_ref[...] = jnp.where(inside, gated, 0.0)
        depth = jnp.zeros((ROWS, 512), F32)
        for k in range(TAPS):
            tap_rows = weights[1, yh, 0, k // 8, (k // 4) % 2][:, 512:].astype(F32)
            at = 8 * ((k // 2) % 2) + 6 + k % 2
            tap = tap_rows[at : at + 1]
            depth = depth + tap * gated_ref[pl.ds(PAD - REACH + k, ROWS), :]
        activated = jax.nn.silu(depth).astype(BF16)
        mixed = mixed + dot_t(activated, mat(1, yh)[:, :512])
    mixed_ref[...] = mixed
    norm_ref[...] = layer_norm(mixed).astype(BF16)


def hidden_of(rows, weights, yh):
    pre = jnp.dot(rows, weights[yh].reshape(D, D), preferred_element_type=F32)
    return jax.nn.silu(pre).astype(BF16)


def out_copies(refs, weights, z, core, sems):
    pairs = []
    for k, ref in enumerate(refs):
        at = lax.rem(z + jnp.where(core == 0, k, Z - k), Z)
        pairs.append((ref, weights.at[:, :, at]))
    return start_copies(pairs, sems)


def other_kernel(offsets, info_ref, own_ref, other_ref, *refs):
    n = len(offsets)
    pieces, out_pieces = refs[:n], refs[n : n + Z]
    hidden_ref, share_ref, first, second, sems, out_sems = refs[n + Z :]
    pairs = crossed_copies(pieces, offsets, first, info_ref[0], info_ref[1], info_ref[2])
    copies = start_copies(pairs, sems)
    later = out_copies(out_pieces, second, info_ref[5], info_ref[2], out_sems)
    for copy in copies:
        copy.wait()
    hidden = [hidden_of(other_ref[...], first, yh) for yh in range(YH)]
    for yh in range(YH):
        hidden_ref[yh] = hidden_of(own_ref[...], first, yh)
    for copy in later:
        copy.wait()
    total = dot_t(hidden[0], second[0].reshape(D, D))
    share_ref[...] = (total + dot_t(hidden[1], second[1].reshape(D, D))).astype(BF16)


def own_kernel(info_ref, hidden_ref, mixed_ref, *refs):
    out_pieces, (out_ref, second, out_sems) = refs[:Z], refs[Z:]
    for copy in out_copies(out_pieces, second, info_ref[5], info_ref[2], out_sems):
        copy.wait()
    total = dot_t(hidden_ref[0], second[0].reshape(D, D))
    total = total + dot_t(hidden_ref[1], second[1].reshape(D, D))
    out_ref[...] = mixed_ref[...] + 0.5 * total


def body(frames, down, proj, glu, conv_taps, conv_out, ffn_in, ffn_out):
    core, x, z = lax.axis_index("c"), lax.axis_index("x"), lax.axis_index("z")
    yh, yl = lax.axis_index("yh"), lax.axis_index("yl")
    y = yh * YL + yl
    where = lax.axis_index(ALL)
    peers = lax.axis_size(ALL)

    proj_half = lax.dynamic_slice_in_dim(proj, yh * 512, 512, 1)
    taps_at = 2 * (lax.rem(z, 2) * 4 + yl * 2 + core)
    taps = lax.dynamic_slice_in_dim(jnp.pad(conv_taps, ((0, 1), (0, 0))), taps_at, 2, 0)
    proj_half = jnp.concatenate([proj_half, taps], axis=0)
    half_a = jnp.stack([glu.reshape(8, 1024), ffn_in[:, :1024]])
    half_b = jnp.stack([jnp.concatenate([conv_out.T, proj_half], axis=1), ffn_in[:, 1024:]])
    mine = jnp.where(core == 0, half_a, half_b)
    theirs = from_offset(jnp.where(core == 0, half_b, half_a), "c", 1)
    out_halves = jnp.stack([ffn_out.T[:, :1024], ffn_out.T[:, 1024:]])
    out_halves = jnp.broadcast_to(out_halves[:, None], (X, YL, CORE, YH, 8, D))
    out_plane = lax.all_to_all(
        out_halves.reshape(-1, 8, D), ("x", "yl", "c", "yh"), 0, 0, tiled=True
    )
    block = jnp.concatenate(
        [jnp.where(core == 0, mine, theirs), jnp.where(core == 0, theirs, mine)], axis=1
    )
    info = jnp.stack(
        [x, y, core, jnp.where(where == 0, PAD, 0),
         jnp.where(where == peers - 1, PAD + ROWS, WITH_HALO), z, jnp.where(core == 0, y, x)]
    ).astype(jnp.int32)

    pieces = spread_z(block, core)

    def plan_z(info_ref):
        steps = []
        for i, (k, _, rows, _) in enumerate(pieces):
            for j in range(abs(rows)):
                at = lax.rem(info_ref[5] + k + (j if rows > 0 else -j), Z)
                steps.append((i, j, 0, (slice(None), at)))
        return steps

    z_blocks, out_plane = lax.optimization_barrier(([p[3] for p in pieces], out_plane))
    out_plane = out_plane.reshape(X, YL, CORE, YH, 8, D).transpose(3, 0, 1, 2, 4, 5)
    out_pieces = [out_plane.reshape(YH, X, YL, 16, D)]

    def more_out(steps):
        for _ in range(steps):
            out_pieces.append(one_way_z(out_pieces[-1]))

    more_out(2)
    (first,) = place(z_blocks, info, plan_z, [(2, Z, 16, D)])
    middle = middle_ring(first)

    def plan_middle(info_ref):
        return [
            (i, half, half, lax.rem(info_ref[6] + k, 4))
            for half in range(2)
            for i, (k, *_) in enumerate(middle)
        ]

    frames, first = lax.optimization_barrier((frames, first))
    pairs = [(i, i ^ 1) for i in range(peers)]
    start, end = frames[:EDGE], frames[-EDGE:]
    near = lax.ppermute(jnp.where(yh == 0, end, start), ALL, pairs)
    pairs = [(i, j) for i in range(peers) if 0 <= (j := i + 2 * (i % 2) - 1) < peers]
    far = lax.ppermute(jnp.where(yh == 0, start, end), ALL, pairs)
    before, after = jnp.where(yh == 0, far, near), jnp.where(yh == 0, near, far)
    blocks, out_pieces[-1], before, after = lax.optimization_barrier(
        ([p[3] for p in middle], out_pieces[-1], before, after)
    )
    front_block, in_block = place(blocks, info, plan_middle, [(4, Z, 16, D)] * 2)
    front_low, front_high, front_rest = last_ring(front_block)
    other_own = from_offset(front_block, "c", 1)
    reduced = pl.pallas_call(
        reduce_kernel,
        out_shape=jax.ShapeDtypeStruct((WITH_HALO, D), BF16),
        in_specs=[VMEM] * 4,
        out_specs=VMEM,
        scratch_shapes=[pltpu.VMEM((DIN // 128, 2 * EDGE + frames.shape[0], 128), F32)],
        compiler_params=params(12),
        cost_estimate=cost(2 * WITH_HALO * DIN * D, 10**7),
    )(before, frames, after, down)
    more_out(1)
    in_block, reduced = lax.optimization_barrier((in_block, reduced))
    in_low, in_high, in_rest = last_ring(in_block)
    out_pieces[-1], other_own = lax.optimization_barrier((out_pieces[-1], other_own))
    more_out(1)
    front_low, front_high, out_pieces[-1] = lax.optimization_barrier(
        (front_low, front_high, out_pieces[-1])
    )
    front_pieces = front_rest(front_low, front_high)
    more_out(1)
    in_low, in_high, out_pieces[-1], next_blocks = lax.optimization_barrier(
        (in_low, in_high, out_pieces[-1], [p[3] for p in front_pieces[1:3]])
    )
    front_other = [other_own] + [from_offset(block, "c", 1) for block in next_blocks]
    in_low, in_high, _ = lax.optimization_barrier(
        (in_low, in_high, [p[3] for p in front_pieces[3:]])
    )
    in_pieces = in_rest(in_low, in_high)
    more_out(1)
    out_first, _ = lax.optimization_barrier((out_pieces[0], out_pieces[4]))
    out_pieces.append(one_way_z(out_first, up_core=1))
    front_other += [from_offset(p, "c", 1) for *_, p in front_pieces[3:]]

    offsets = [p[:3] for p in front_pieces]
    mixed, norm = pl.pallas_call(
        functools.partial(front_kernel, offsets),
        out_shape=(jax.ShapeDtypeStruct((ROWS, D), F32), jax.ShapeDtypeStruct((ROWS, D), BF16)),
        in_specs=[SMEM, VMEM] + [ANY] * (2 * len(offsets)),
        out_specs=(VMEM, VMEM),
        scratch_shapes=[
            pltpu.VMEM((2, YH, X, Z, YL, 16, D), BF16),
            pltpu.VMEM((WITH_HALO, 512), F32),
            pltpu.SemaphoreType.DMA((2, 16)),
        ],
        compiler_params=params(),
        cost_estimate=cost(2 * WITH_HALO * D * D * 4, 10**7),
    )(info, reduced, *[p[3] for p in front_pieces], *front_other)

    offsets = [p[:3] for p in in_pieces]
    in_pieces = [p[3] for p in in_pieces]
    norm, in_pieces, out_pieces[7] = lax.optimization_barrier((norm, in_pieces, out_pieces[7]))
    norm_other = from_offset(norm, "c", 1)
    whole = pltpu.VMEM((YH, X, Z, YL, 16, D), BF16)
    hidden, share = pl.pallas_call(
        functools.partial(other_kernel, offsets),
        out_shape=(
            jax.ShapeDtypeStruct((YH, ROWS, D), BF16),
            jax.ShapeDtypeStruct((ROWS, D), BF16),
        ),
        in_specs=[SMEM, VMEM, VMEM] + [ANY] * (len(offsets) + Z),
        out_specs=(VMEM, VMEM),
        scratch_shapes=[
            whole, whole, pltpu.SemaphoreType.DMA((16,)), pltpu.SemaphoreType.DMA((Z,))
        ],
        compiler_params=params(),
        cost_estimate=cost(6 * 2 * ROWS * D * D, 10**7),
    )(info, norm, norm_other, *in_pieces, *out_pieces)
    share = from_offset(share, "c", 1)
    own = pl.pallas_call(
        own_kernel,
        out_shape=jax.ShapeDtypeStruct((ROWS, D), F32),
        in_specs=[SMEM, VMEM, VMEM] + [ANY] * Z,
        out_specs=VMEM,
        scratch_shapes=[whole, pltpu.SemaphoreType.DMA((Z,))],
        compiler_params=params(),
        cost_estimate=cost(2 * 2 * ROWS * D * D, 10**7),
    )(info, hidden, mixed, *out_pieces)
    return (own + 0.5 * share.astype(F32)).astype(BF16)


def solution(mesh):
    parts = Mesh(mesh.devices.reshape(X, Z, YL, CORE, YH), ALL)
    return jax.shard_map(
        body,
        mesh=parts,
        in_specs=(
            P(ALL, None),
            P(),
            P(WIDE, None),
            P(WIDE, None, "yh"),
            P(None, "yh"),
            P("yh", WIDE),
            P(WIDE, "yh"),
            P("yh", WIDE),
        ),
        out_specs=P(ALL, None),
        check_vma=False,
    )
```
